256 devices in a mesh: theta: 32 (over x_hi, z, core), xr: 8 (over x_lo, y).
Axes of the slice: x: 4 (x_hi: 2, x_lo: 2; x = x_hi * 2 + x_lo), y: 4, z: 8, core: 2. Of those that a mesh axis runs over, the one named last changes fastest.
Arguments:
- state: float32 [3, 2, 5, 256, 64, 128], P(None, None, None, 'theta', 'xr'), may hold values from -6 to 6
- source: float32 [3, 2, 5, 256, 64, 128], P(None, None, None, 'theta', 'xr'), may hold values from -6 to 6
- sigma: float32 [256, 64, 128], P('theta', 'xr'), may hold values from 0.25 to 4
- stagger: int32 [64], P('theta'), may hold values from 0 to 3
- a_theta: float32 [4, 5, 5], replicated, may hold values from -2.5 to 2.5
- a_axial: float32 [5, 5], replicated, may hold values from -2.5 to 2.5
- a_radial: float32 [5, 5], replicated, may hold values from -2.5 to 2.5
- mode_order: int32 [3, 128], replicated, may hold values from -32 to 32
- mode_radial: int32 [3, 128], replicated, may hold values from 0 to 7
- mode_plane: int32 [3, 128], replicated, may hold values from 0 to 1
- gust: float32 [3, 2, 128], replicated, may hold values from -6 to 6
- l_rows: float32 [2, 5], replicated, may hold values from -4 to 4
- r_cols: float32 [2, 5], replicated, may hold values from -4 to 4
Outputs:
- fields: float32 [3, 2, 5, 256, 64, 128], P(None, None, None, 'theta', 'xr')
- amplitudes: float32 [3, 2, 2, 128], replicated
The draws below stay inside these ranges and needn't reach their ends.
Inputs may be any that keep to these rules, and one draw needn't show every extreme that they name: `mode_plane`: 0 names the inlet plane, 1 the exit plane.
All inputs are finite; a program needn't handle non-finite values.
Results may differ from the reference program's by a relative error of at most 0.0003.
Values sent between devices are 32-bit elements; how exact they have to be, the bound alone decides.
No kernel may reach another device: no remote copies, remote signals or barrier semaphores. Data moves between devices by JAX's collectives and lax.ppermute only.
A program may use at most 64 MiB of HBM per device.

```python
import math
import jax
import jax.numpy as jnp
from jax import lax

H = 3
V = 5
STAGGERS = 4
CPP = 4
NR = 128
MODES = 128
M_MAX = 32
NRAD = 8
PASSAGES = 64
NT = 256
NX = 64


def set_ends(array, stream_key, smallest, top_value):
    index_at = [jax.random.randint(jax.random.fold_in(stream_key, axis), (), 0, length) for axis, length in enumerate(array.shape)]
    longest = array.shape.index(max(array.shape))
    neighbour = index_at[:longest] + [(index_at[longest] + 1) % array.shape[longest]] + index_at[longest + 1:]
    return array.at[tuple(index_at)].set(smallest).at[tuple(neighbour)].set(top_value)


def steps_of(stream_key, dims, shards, low, top_value):
    def one(axis_at, blocks):
        steps = jax.random.uniform(jax.random.fold_in(jax.random.fold_in(stream_key, 6), axis_at), (blocks,), jnp.float32, low / len(shards), top_value / len(shards))
        return jnp.repeat(jnp.exp(steps), dims[axis_at] // blocks).reshape((-1,) + (1,) * (len(dims) - axis_at - 1))

    level = one(*shards[0])
    for cut in shards[1:]:
        level = level * one(*cut)
    return level


def bell_draw(key, dims, deviation, reach, split=(), dtype=jnp.bfloat16):
    entries = deviation * jax.random.normal(key, dims, jnp.float32)
    if split:
        entries = entries * steps_of(key, dims, split, -0.22, 0.18)
    return jnp.clip(entries, -reach, reach).astype(dtype)


def setup_inputs(seed: int = 0) -> dict:
    streams_of = jax.random.split(jax.random.key(seed), 14)
    return {
        "state": bell_draw(streams_of[0], (H, 2, V, NT, NX, NR), 1.0, 6.0, ((3, 32), (4, 8)), jnp.float32),
        "source": bell_draw(streams_of[1], (H, 2, V, NT, NX, NR), 1.0, 6.0, ((3, 32), (4, 8)), jnp.float32),
        "sigma": jnp.clip(jnp.exp(math.log(4.0) - 2.7725887 * jax.random.uniform(streams_of[2], (NT, NX, NR), jnp.float32) ** steps_of(streams_of[2], (NT, NX, NR), ((0, 32), (1, 8)), -0.2, 0.2)), 0.25, 4.0),
        "stagger": set_ends(jax.random.randint(streams_of[3], (PASSAGES,), 0, STAGGERS), jax.random.fold_in(streams_of[3], 1), 0, STAGGERS - 1).astype(jnp.int32),
        "a_theta": bell_draw(streams_of[4], (STAGGERS, V, V), V ** -0.5, 2.5, (), jnp.float32),
        "a_axial": bell_draw(streams_of[5], (V, V), V ** -0.5, 2.5, (), jnp.float32),
        "a_radial": bell_draw(streams_of[6], (V, V), V ** -0.5, 2.5, (), jnp.float32),
        "mode_order": set_ends(jax.random.randint(streams_of[7], (H, MODES), 0 - M_MAX, M_MAX + 1), jax.random.fold_in(streams_of[7], 1), 0 - M_MAX, M_MAX).astype(jnp.int32),
        "mode_radial": set_ends(jax.random.randint(streams_of[8], (H, MODES), 0, NRAD), jax.random.fold_in(streams_of[8], 1), 0, NRAD - 1).astype(jnp.int32),
        "mode_plane": set_ends(jax.random.randint(streams_of[9], (H, MODES), 0, 2), jax.random.fold_in(streams_of[9], 1), 0, 1).astype(jnp.int32),
        "gust": bell_draw(streams_of[10], (H, 2, MODES), 1.0, 6.0, (), jnp.float32),
        "l_rows": bell_draw(streams_of[11], (2, V), 1.0, 4.0, (), jnp.float32),
        "r_cols": bell_draw(streams_of[12], (2, V), 1.0, 4.0, (), jnp.float32),
    }


courant = 0.5
viscosity = 0.1
base_frequency = 0.5
highest = lax.Precision.HIGHEST

def reference(state, source, sigma, stagger, a_theta, a_axial, a_radial, mode_order, mode_radial, mode_plane, gust, l_rows, r_cols):
    cells = jnp.arange(NT).astype(jnp.int32)
    cell_matrix = a_theta[stagger[cells // CPP]]
    step_size = courant / (1.0 + sigma)
    scale = 1.0 / math.sqrt(NT * NR)
    radial_pos = jnp.arange(NR).astype(jnp.float32) + 0.5

    def residual(field, freq, forcing):
        diff_theta = (jnp.roll(field, -1, 2) - jnp.roll(field, 1, 2)) * 0.5
        lap_theta = jnp.roll(field, -1, 2) + jnp.roll(field, 1, 2) - 2.0 * field
        padded_x = jnp.pad(field, ((0, 0), (0, 0), (0, 0), (1, 1), (0, 0)))
        diff_axial = (padded_x[:, :, :, 2:] - padded_x[:, :, :, :-2]) * 0.5
        lap_axial = padded_x[:, :, :, 2:] + padded_x[:, :, :, :-2] - 2.0 * field
        padded_r = jnp.pad(field, ((0, 0), (0, 0), (0, 0), (0, 0), (1, 1)))
        diff_radial = (padded_r[..., 2:] - padded_r[..., :-2]) * 0.5
        lap_radial = padded_r[..., 2:] + padded_r[..., :-2] - 2.0 * field
        turned = jnp.stack([-field[1], field[0]])
        flux = jnp.einsum('tvw,pwtxr->pvtxr', cell_matrix, diff_theta, precision=highest)
        flux = flux + jnp.einsum('vw,pwtxr->pvtxr', a_axial, diff_axial, precision=highest)
        flux = flux + jnp.einsum('vw,pwtxr->pvtxr', a_radial, diff_radial, precision=highest)
        return freq * turned + flux - viscosity * (lap_theta + lap_axial + lap_radial) + sigma * field - forcing

    def one_harmonic(items):
        field, forcing, freq, orders, radial, planes, target = items
        first = field - 0.5 * step_size * residual(field, freq, forcing)
        second = field - step_size * residual(first, freq, forcing)
        inlet = jnp.einsum('v,pvtr->ptr', l_rows[0], second[:, :, :, 0, :], precision=highest)
        outlet = jnp.einsum('v,pvtr->ptr', l_rows[1], second[:, :, :, NX - 1, :], precision=highest)
        plane_values = jnp.stack([inlet, outlet])
        angle = 2.0 * math.pi * jnp.mod(orders[:, None] * cells[None, :], NT).astype(jnp.float32) / NT
        cos_table = jnp.cos(angle)
        sin_table = jnp.sin(angle)
        radial_table = jnp.where(radial[:, None] == 0, 1.0, math.sqrt(2.0) * jnp.cos(math.pi * radial[:, None].astype(jnp.float32) * radial_pos[None, :] / NR))
        projected = jnp.einsum('bptr,kr->bptk', plane_values, radial_table, precision=highest)
        amp_real = scale * (jnp.einsum('btk,kt->bk', projected[:, 0], cos_table, precision=highest) + jnp.einsum('btk,kt->bk', projected[:, 1], sin_table, precision=highest))
        amp_imag = scale * (jnp.einsum('btk,kt->bk', projected[:, 1], cos_table, precision=highest) - jnp.einsum('btk,kt->bk', projected[:, 0], sin_table, precision=highest))
        weight = (planes[None, :] == jnp.arange(2)[:, None]).astype(jnp.float32)
        miss_real = weight * (amp_real - target[0][None, :])
        miss_imag = weight * (amp_imag - target[1][None, :])
        coef_real = miss_real[:, :, None] * cos_table[None] - miss_imag[:, :, None] * sin_table[None]
        coef_imag = miss_real[:, :, None] * sin_table[None] + miss_imag[:, :, None] * cos_table[None]
        corr_real = jnp.einsum('bkt,kr->btr', coef_real, radial_table, precision=highest)
        corr_imag = jnp.einsum('bkt,kr->btr', coef_imag, radial_table, precision=highest)
        correction = scale * jnp.stack([corr_real, corr_imag], axis=1)
        second = second.at[:, :, :, 0, :].add(-r_cols[0][None, :, None, None] * correction[0][:, None])
        second = second.at[:, :, :, NX - 1, :].add(-r_cols[1][None, :, None, None] * correction[1][:, None])
        measured = jnp.stack([weight * amp_real, weight * amp_imag], axis=1)
        return (second, measured)
    freqs = base_frequency * (1.0 + jnp.arange(H).astype(jnp.float32))
    fields, amplitudes = lax.map(one_harmonic, (state, source, freqs, mode_order, mode_radial, mode_plane, gust))
    return (fields, amplitudes)
```

```python
import functools
import math

import jax
import jax.numpy as jnp
from jax import lax
from jax.experimental import pallas as pl
from jax.experimental.pallas import tpu as pltpu
from jax.sharding import PartitionSpec as P

courant = 0.5
viscosity = 0.1
base_frequency = 0.5
highest = lax.Precision.HIGHEST
VM = pltpu.VMEM
SM = pltpu.SMEM


def spec(space):
    return pl.BlockSpec(memory_space=space)


def params():
    return pltpu.CompilerParams(vmem_limit_bytes=40 * 1024 * 1024)


def write_faces(place, u_ref, te_ref, to_ref, xe_ref, xo_ref):
    nhp, nvar = u_ref.shape[0], u_ref.shape[1]
    todd = lax.rem(place[0], 2)
    xodd = lax.rem(place[1], 2)
    for out_ref, layer in ((te_ref, 1 - todd), (to_ref, todd)):
        start = pl.multiple_of(layer * 56, 8)
        out_ref[...] = u_ref[:, :, pl.ds(start, 8), :]
    for out_ref, row in ((xe_ref, 1 - xodd), (xo_ref, xodd)):
        for i in range(nhp):
            for v in range(nvar):
                out_ref[i, v] = u_ref[i, v, pl.ds(row * 7, 8, stride=8), :]


def pack_kernel(place, u_ref, te_ref, to_ref, xe_ref, xo_ref):
    write_faces(place, u_ref, te_ref, to_ref, xe_ref, xo_ref)


def step(factor, place, stagger, a_theta, a_axial, a_radial, u_ref, base_ref, src_ref, sig_ref, te, to, xe, xo, out_ref):
    nhp, nvar, rows, nr = u_ref.shape
    tcells = rows // 8
    cpp = tcells // stagger.shape[0]
    todd = lax.rem(place[0], 2) == 1
    xodd = lax.rem(place[1], 2) == 1
    shape = (nhp, 8, nr)
    row = lax.broadcasted_iota(jnp.int32, shape, 1)
    lane = lax.broadcasted_iota(jnp.int32, shape, 2)
    axial = [[0.5 * a_axial[v, w] for w in range(nvar)] for v in range(nvar)]
    radial = [[0.5 * a_radial[v, w] for w in range(nvar)] for v in range(nvar)]
    for t in range(tcells):
        setting = stagger[t // cpp]
        tile = slice(8 * t, 8 * t + 8)
        sig = sig_ref[tile, :][None]
        own = sig + 6.0 * viscosity
        scaled = (factor * courant) / (1.0 + sig)
        acc = [None] * nvar
        for w in range(nvar):
            u = u_ref[:, w, tile, :]
            if t == 0:
                tm = jnp.where(todd, te[:, w], to[:, w])
            else:
                tm = u_ref[:, w, 8 * t - 8 : 8 * t, :]
            if t == tcells - 1:
                tp = jnp.where(todd, to[:, w], te[:, w])
            else:
                tp = u_ref[:, w, 8 * t + 8 : 8 * t + 16, :]
            e = xe[:, w, t : t + 1, :]
            o = xo[:, w, t : t + 1, :]
            xlo = jnp.where(xodd, e, o)
            xhi = jnp.where(xodd, o, e)
            xm = jnp.where(row == 0, jnp.broadcast_to(xlo, shape), pltpu.roll(u, 1, 1))
            xp = jnp.where(row == 7, jnp.broadcast_to(xhi, shape), pltpu.roll(u, 7, 1))
            rm = jnp.where(lane == 0, 0.0, pltpu.roll(u, 1, 2))
            rp = jnp.where(lane == nr - 1, 0.0, pltpu.roll(u, nr - 1, 2))
            dt_, dx_, dr_ = tp - tm, xp - xm, rp - rm
            near = ((tp + tm) + (xp + xm)) + (rp + rm)
            turned = []
            for h in range(nhp // 2):
                freq = base_frequency * (1.0 + h)
                turned.append(-freq * u[2 * h + 1 : 2 * h + 2])
                turned.append(freq * u[2 * h : 2 * h + 1])
            local_part = (own * u - viscosity * near) + (jnp.concatenate(turned, axis=0) - src_ref[:, w, tile, :])
            for v in range(nvar):
                flux = (0.5 * a_theta[setting, v, w]) * dt_ + axial[v][w] * dx_ + radial[v][w] * dr_
                if v == w:
                    flux = flux + local_part
                acc[v] = flux if acc[v] is None else acc[v] + flux
        for v in range(nvar):
            out_ref[:, v, tile, :] = base_ref[:, v, tile, :] - scaled * acc[v]


def first_kernel(
    place, stagger, a_theta, a_axial, a_radial, u_ref, src_ref, sig_ref, te, to, xe, xo, out_ref, te2, to2, xe2, xo2
):
    step(0.5, place, stagger, a_theta, a_axial, a_radial, u_ref, u_ref, src_ref, sig_ref, te, to, xe, xo, out_ref)
    write_faces(place, out_ref, te2, to2, xe2, xo2)


def tables(place, order, tcells, tdevices):
    nharm, nmode = order.shape
    total = tcells * tdevices
    cell = place[0] * tcells + lax.broadcasted_iota(jnp.int32, (tcells, nmode), 0)
    cos, sin = [], []
    for h in range(nharm):
        turns = lax.rem(order[h : h + 1, :] * cell + 64 * total, total)
        angle = 2.0 * math.pi * turns.astype(jnp.float32) / total
        cos.append(jnp.cos(angle))
        sin.append(jnp.sin(angle))
    return cos, sin


def radial_table(nrad, nr):
    n = lax.broadcasted_iota(jnp.int32, (nrad, nr), 0)
    pos = lax.broadcasted_iota(jnp.int32, (nrad, nr), 1).astype(jnp.float32) + 0.5
    wave = math.sqrt(2.0) * jnp.cos(math.pi * n.astype(jnp.float32) * pos / nr)
    return jnp.where(n == 0, 1.0, wave)


def second_kernel(
    tdevices,
    xdevices,
    nrad,
    place,
    stagger,
    a_theta,
    a_axial,
    a_radial,
    l_rows,
    u_ref,
    base_ref,
    src_ref,
    sig_ref,
    te,
    to,
    xe,
    xo,
    order,
    radial,
    plane,
    out_ref,
    part_ref,
):
    step(1.0, place, stagger, a_theta, a_axial, a_radial, u_ref, base_ref, src_ref, sig_ref, te, to, xe, xo, out_ref)
    nhp, nvar, rows, nr = out_ref.shape
    nharm, nmode = order.shape
    tcells = rows // 8
    scale = 1.0 / math.sqrt(tcells * tdevices * nr)
    last = (place[1] == xdevices - 1).astype(jnp.int32)
    holds = jnp.logical_or(place[1] == 0, place[1] == xdevices - 1)
    values = []
    for i in range(nhp):
        c = None
        for v in range(nvar):
            term = l_rows[last, v] * out_ref[i, v, pl.ds(last * 7, tcells, stride=8), :]
            c = term if c is None else c + term
        values.append(c)
    values = jnp.concatenate(values, axis=0)
    waves = radial_table(nrad, nr)
    nt = (((1,), (1,)), ((), ()))
    grouped = lax.dot_general(values, waves, nt, precision=highest, preferred_element_type=jnp.float32)
    cos, sin = tables(place, order, tcells, tdevices)
    out = []
    for h in range(nharm):
        pick = (lax.broadcasted_iota(jnp.int32, (nrad, nmode), 0) == radial[h : h + 1, :]).astype(jnp.float32)
        mine = jnp.logical_and(plane[h : h + 1, :] == last, holds)
        both = jnp.dot(
            grouped[2 * tcells * h : 2 * tcells * (h + 1)], pick, precision=highest, preferred_element_type=jnp.float32
        )
        re, im = both[:tcells], both[tcells:]
        part_re = scale * jnp.sum(re * cos[h] + im * sin[h], axis=0, keepdims=True)
        part_im = scale * jnp.sum(im * cos[h] - re * sin[h], axis=0, keepdims=True)
        out.append(jnp.where(mine, part_re, 0.0))
        out.append(jnp.where(mine, part_im, 0.0))
    out.append(jnp.zeros((8 - nhp, nmode), jnp.float32))
    block = jnp.concatenate(out, axis=0)
    for d in range(tdevices):
        part_ref[d] = block


def correct_kernel(
    tdevices, xdevices, nrad, place, r_cols, got_ref, gust, second_ref, order, radial, plane, out_ref, amp_ref
):
    nhp, nvar, rows, nr = out_ref.shape
    nharm, nmode = order.shape
    tcells = rows // 8
    scale = 1.0 / math.sqrt(tcells * tdevices * nr)
    last = (place[1] == xdevices - 1).astype(jnp.int32)
    holds = jnp.logical_or(place[1] == 0, place[1] == xdevices - 1)
    amp = jnp.sum(got_ref[...], axis=0)
    for d in range(xdevices):
        amp_ref[d] = amp
    out_ref[...] = second_ref[...]

    @pl.when(holds)
    def _():
        waves = radial_table(nrad, nr)
        cos, sin = tables(place, order, tcells, tdevices)
        for h in range(nharm):
            pick = (lax.broadcasted_iota(jnp.int32, (nrad, nmode), 0) == radial[h : h + 1, :]).astype(jnp.float32)
            mine = plane[h : h + 1, :] == last
            miss_re = jnp.where(mine, amp[2 * h : 2 * h + 1] - gust[h, 0:1, :], 0.0)
            miss_im = jnp.where(mine, amp[2 * h + 1 : 2 * h + 2] - gust[h, 1:2, :], 0.0)
            coef = jnp.concatenate([miss_re * cos[h] - miss_im * sin[h], miss_re * sin[h] + miss_im * cos[h]], axis=0)
            nt = (((1,), (1,)), ((), ()))
            grouped = lax.dot_general(coef, pick, nt, precision=highest, preferred_element_type=jnp.float32)
            q = scale * jnp.dot(grouped, waves, precision=highest, preferred_element_type=jnp.float32)
            for p in range(2):
                for v in range(nvar):
                    at = pl.ds(last * 7, tcells, stride=8)
                    out_ref[2 * h + p, v, at, :] = (
                        second_ref[2 * h + p, v, at, :] - r_cols[last, v] * q[p * tcells : (p + 1) * tcells]
                    )


def local(
    state, source, sigma, stagger, a_theta, a_axial, a_radial, mode_order, mode_radial, mode_plane, gust, l_rows, r_cols
):
    nharm, two, nvar, ctheta, caxial, nradial = state.shape
    nhp = nharm * two
    tdev, xdev = lax.axis_size("theta"), lax.axis_size("xr")
    nrad = 8
    block = (nhp, nvar, ctheta * caxial, nradial)
    u = state.reshape(block)
    src = source.reshape(block)
    sig = sigma.reshape(ctheta * caxial, nradial)
    place = jnp.stack([lax.axis_index("theta"), lax.axis_index("xr")]).astype(jnp.int32)
    f32 = jnp.float32
    face = jax.ShapeDtypeStruct((nhp, nvar, 8, nradial), f32)
    whole = jax.ShapeDtypeStruct(block, f32)

    even_t = [(i, i ^ 1) for i in range(tdev)]
    odd_t = [(i, (i + 1) % tdev if i % 2 else (i - 1) % tdev) for i in range(tdev)]
    even_x = [(i, i ^ 1) for i in range(xdev)]
    odd_x = [(i, i + 1 if i % 2 else i - 1) for i in range(1, xdev - 1)]

    def swap(te, to, xe, xo):
        return (
            lax.ppermute(te, "theta", even_t),
            lax.ppermute(to, "theta", odd_t),
            lax.ppermute(xe, "xr", even_x),
            lax.ppermute(xo, "xr", odd_x),
        )

    faces = pl.pallas_call(
        pack_kernel,
        in_specs=[spec(SM), spec(VM)],
        out_specs=[spec(VM)] * 4,
        out_shape=[face] * 4,
        compiler_params=params(),
        name="pack_faces",
    )(place, u)
    faces = swap(*faces)
    first, *faces = pl.pallas_call(
        first_kernel,
        in_specs=[spec(SM)] * 5 + [spec(VM)] * 7,
        out_specs=[spec(VM)] * 5,
        out_shape=[whole] + [face] * 4,
        compiler_params=params(),
        name="first_step",
    )(place, stagger, a_theta, a_axial, a_radial, u, src, sig, *faces)
    faces = swap(*faces)
    second, part = pl.pallas_call(
        functools.partial(second_kernel, tdev, xdev, nrad),
        in_specs=[spec(SM)] * 6 + [spec(VM)] * 11,
        out_specs=[spec(VM)] * 2,
        out_shape=[whole, jax.ShapeDtypeStruct((tdev, 8, mode_order.shape[1]), f32)],
        compiler_params=params(),
        name="second_step",
    )(
        place, stagger, a_theta, a_axial, a_radial, l_rows, first, u, src, sig, *faces, mode_order, mode_radial, mode_plane
    )
    got = lax.all_to_all(part, "theta", 0, 0, tiled=True)
    fields, amp = pl.pallas_call(
        functools.partial(correct_kernel, tdev, xdev, nrad),
        in_specs=[spec(SM)] * 2 + [spec(VM)] * 6,
        out_specs=[spec(VM)] * 2,
        out_shape=[whole, jax.ShapeDtypeStruct((xdev, 8, mode_order.shape[1]), f32)],
        compiler_params=params(),
        name="correct_planes",
    )(place, r_cols, got, gust, second, mode_order, mode_radial, mode_plane)
    amp = lax.all_to_all(amp, "xr", 0, 0, tiled=True)
    amp = jnp.sum(amp, axis=0)[:nhp].reshape(nharm, 1, two, -1)
    weight = (mode_plane[:, None, None, :] == jnp.arange(2)[None, :, None, None]).astype(f32)
    return fields.reshape(state.shape), weight * amp


def solution(mesh):
    placed = (
        P(None, None, None, "theta", "xr", None),
        P(None, None, None, "theta", "xr", None),
        P("theta", "xr", None),
        P("theta"),
        P(),
        P(),
        P(),
        P(),
        P(),
        P(),
        P(),
        P(),
        P(),
    )
    return jax.shard_map(
        local,
        mesh=mesh,
        in_specs=placed,
        out_specs=(P(None, None, None, "theta", "xr", None), P()),
        check_vma=False,
    )
```

```python
import functools
import math

import jax
import jax.numpy as jnp
from jax import lax
from jax.experimental import pallas as pl
from jax.experimental.pallas import tpu as pltpu
from jax.sharding import PartitionSpec as P

courant = 0.5
viscosity = 0.1
base_frequency = 0.5
highest = lax.Precision.HIGHEST
VM = pltpu.VMEM
SM = pltpu.SMEM
planes_first = True
wide = ("pack_faces", "plane_part", "mode_tables", "first_step")


def spec(space):
    return pl.BlockSpec(memory_space=space)


def params(name):
    size = 60 if name in wide else 16
    return pltpu.CompilerParams(vmem_limit_bytes=size * 1024 * 1024)


def write_faces(place, u_ref, te_ref, to_ref, xe_ref, xo_ref):
    nhp, nvar = u_ref.shape[0], u_ref.shape[1]
    todd = lax.rem(place[0], 2)
    xodd = lax.rem(place[1], 2)
    for out_ref, layer in ((te_ref, 1 - todd), (to_ref, todd)):
        start = pl.multiple_of(layer * 56, 8)
        out_ref[0:nhp] = u_ref[:, :, pl.ds(start, 8), :]
    for out_ref, row in ((xe_ref, 1 - xodd), (xo_ref, xodd)):
        for i in range(nhp):
            for v in range(nvar):
                out_ref[i, v] = u_ref[i, v, pl.ds(row * 7, 8, stride=8), :]


def pack_kernel(place, stagger, u_ref, sig_ref, te_ref, to_ref, xe_ref, xo_ref):
    write_faces(place, u_ref, te_ref, to_ref, xe_ref, xo_ref)
    nhp = u_ref.shape[0]
    nr = u_ref.shape[3]
    npass = stagger.shape[0]
    todd = lax.rem(place[0], 2)
    for out_ref, layer in ((te_ref, 1 - todd), (to_ref, todd)):
        start = pl.multiple_of(layer * 48, 8)
        out_ref[nhp, 0] = sig_ref[pl.ds(start, 8), :]
        out_ref[nhp, 1] = sig_ref[pl.ds(start + 8, 8), :]
        setting = stagger[layer * (npass - 1)].astype(jnp.float32)
        for i in range(2, out_ref.shape[1]):
            out_ref[nhp, i] = jnp.full((8, nr), setting, jnp.float32)


def step(factor, place, stagger, a_theta, a_axial, a_radial, u_ref, base_ref, src_ref, sig_ref, te, to, xe, xo, out_ref):
    nhp, nvar, rows, nr = u_ref.shape
    tcells = rows // 8
    cpp = tcells // stagger.shape[0]
    todd = lax.rem(place[0], 2) == 1
    xodd = lax.rem(place[1], 2) == 1
    shape = (nhp, 8, nr)
    row = lax.broadcasted_iota(jnp.int32, shape, 1)
    lane = lax.broadcasted_iota(jnp.int32, shape, 2)
    axial = [[0.5 * a_axial[v, w] for w in range(nvar)] for v in range(nvar)]
    radial = [[0.5 * a_radial[v, w] for w in range(nvar)] for v in range(nvar)]
    for t in range(tcells):
        setting = stagger[t // cpp]
        tile = slice(8 * t, 8 * t + 8)
        sig = sig_ref[tile, :][None]
        own = sig + 6.0 * viscosity
        scaled = (factor * courant) / (1.0 + sig)
        acc = [None] * nvar
        for w in range(nvar):
            u = u_ref[:, w, tile, :]
            if t == 0:
                tm = jnp.where(todd, te[0:nhp, w], to[0:nhp, w])
            else:
                tm = u_ref[:, w, 8 * t - 8 : 8 * t, :]
            if t == tcells - 1:
                tp = jnp.where(todd, to[0:nhp, w], te[0:nhp, w])
            else:
                tp = u_ref[:, w, 8 * t + 8 : 8 * t + 16, :]
            e = xe[:, w, t : t + 1, :]
            o = xo[:, w, t : t + 1, :]
            xlo = jnp.where(xodd, e, o)
            xhi = jnp.where(xodd, o, e)
            xm = jnp.where(row == 0, jnp.broadcast_to(xlo, shape), pltpu.roll(u, 1, 1))
            xp = jnp.where(row == 7, jnp.broadcast_to(xhi, shape), pltpu.roll(u, 7, 1))
            rm = jnp.where(lane == 0, 0.0, pltpu.roll(u, 1, 2))
            rp = jnp.where(lane == nr - 1, 0.0, pltpu.roll(u, nr - 1, 2))
            dt_, dx_, dr_ = tp - tm, xp - xm, rp - rm
            near = ((tp + tm) + (xp + xm)) + (rp + rm)
            turned = []
            for h in range(nhp // 2):
                freq = base_frequency * (1.0 + h)
                turned.append(-freq * u[2 * h + 1 : 2 * h + 2])
                turned.append(freq * u[2 * h : 2 * h + 1])
            local_part = (own * u - viscosity * near) + (jnp.concatenate(turned, axis=0) - src_ref[:, w, tile, :])
            for v in range(nvar):
                flux = (0.5 * a_theta[setting, v, w]) * dt_ + axial[v][w] * dx_ + radial[v][w] * dr_
                if v == w:
                    flux = flux + local_part
                acc[v] = flux if acc[v] is None else acc[v] + flux
        for v in range(nvar):
            out_ref[:, v, tile, :] = base_ref[:, v, tile, :] - scaled * acc[v]


def first_kernel(
    place, stagger, a_theta, a_axial, a_radial, u_ref, src_ref, sig_ref, te, to, xe, xo, after, out_ref, te2, to2, xe2, xo2
):
    step(0.5, place, stagger, a_theta, a_axial, a_radial, u_ref, u_ref, src_ref, sig_ref, te, to, xe, xo, out_ref)
    write_faces(place, out_ref, te2, to2, xe2, xo2)


def second_kernel(
    place, stagger, a_theta, a_axial, a_radial, u_ref, base_ref, src_ref, sig_ref, te, to, xe, xo, out_ref
):
    step(1.0, place, stagger, a_theta, a_axial, a_radial, u_ref, base_ref, src_ref, sig_ref, te, to, xe, xo, out_ref)


def table_kernel(tdevices, place, order, radial, cos_ref, sin_ref, wave_ref, pick_ref):
    nharm, nmode = order.shape
    tcells = 8
    total = tcells * tdevices
    row = lax.broadcasted_iota(jnp.int32, (2 * tcells, nmode), 0)
    cell = place[0] * tcells + jnp.where(row < 12, row, row - 16)
    nrad, nr = wave_ref.shape
    wave_ref[...] = radial_table(nrad, nr)
    for h in range(nharm):
        turns = lax.rem(order[h : h + 1, :] * cell + 64 * total, total)
        angle = 2.0 * math.pi * turns.astype(jnp.float32) / total
        cos_ref[h] = jnp.cos(angle)
        sin_ref[h] = jnp.sin(angle)
        n = lax.broadcasted_iota(jnp.int32, (nrad, nmode), 0)
        pick_ref[h] = (n == radial[h : h + 1, :]).astype(jnp.float32)


def radial_table(nrad, nr):
    n = lax.broadcasted_iota(jnp.int32, (nrad, nr), 0)
    pos = lax.broadcasted_iota(jnp.int32, (nrad, nr), 1).astype(jnp.float32) + 0.5
    wave = math.sqrt(2.0) * jnp.cos(math.pi * n.astype(jnp.float32) * pos / nr)
    return jnp.where(n == 0, 1.0, wave)


def turn(u):
    out = []
    for h in range(u.shape[0] // 2):
        freq = base_frequency * (1.0 + h)
        out.append(-freq * u[2 * h + 1 : 2 * h + 2])
        out.append(freq * u[2 * h : 2 * h + 1])
    return jnp.concatenate(out, axis=0)


def plane_part(last, tdevices, stagger, a_theta, a_axial, a_radial, l_rows, u_ref, src_ref, sig_ref, lo, hi, refs):
    plane, cos_ref, sin_ref, wave_ref, pick_ref, part_ref = refs
    nhp, nvar, rows, nr = u_ref.shape
    nharm, nmode = plane.shape
    nset = a_theta.shape[0]
    scale = 1.0 / math.sqrt(8 * tdevices * nr)
    shape = (nhp, 8, nr)
    row = lax.broadcasted_iota(jnp.int32, shape, 1)
    lane = lax.broadcasted_iota(jnp.int32, shape, 2)
    row1, row2 = row[0], lax.broadcasted_iota(jnp.int32, (8, nr), 0)
    side = (1 - 2 * last).astype(jnp.float32)
    at = [last * 7 + j * (1 - 2 * last) for j in range(3)]

    def own_rows(ref, v, j):
        return jnp.stack([ref[i, v, pl.ds(at[j], 8, stride=8), :] for i in range(nhp)])

    def shift_r(u):
        return (
            jnp.where(lane == 0, 0.0, pltpu.roll(u, 1, 2)),
            jnp.where(lane == nr - 1, 0.0, pltpu.roll(u, nr - 1, 2)),
        )

    def row_of(face, i, j):
        return jnp.broadcast_to(face(i, pl.ds(at[j], 1)), (8, nr))

    settings = jnp.where(row2 < 4, hi(2, slice(0, 8)), lo(2, slice(0, 8)))
    table = [[None] * nvar for _ in range(nvar)]
    outer = [[None] * nvar for _ in range(nvar)]
    for v in range(nvar):
        for w in range(nvar):
            table[v][w] = jnp.where(row2 < 4, 0.5 * a_theta[stagger[0], v, w], 0.5 * a_theta[stagger[1], v, w])[None]
            value = jnp.full((8, nr), 0.5 * a_theta[nset - 1, v, w], jnp.float32)
            for s in range(nset - 1):
                value = jnp.where(settings == float(s), 0.5 * a_theta[s, v, w], value)
            outer[v][w] = value[None]
    axial = [[0.5 * side * a_axial[v, w] for w in range(nvar)] for v in range(nvar)]
    radial = [[0.5 * a_radial[v, w] for w in range(nvar)] for v in range(nvar)]
    weight = [l_rows[last, v] for v in range(nvar)]

    sig, sig_out, step_in, step_out = [], [], [], []
    for j in range(2):
        sig.append(sig_ref[pl.ds(at[j], 8, stride=8), :][None])
        edge = jnp.where(row2 == 0, row_of(hi, 0, j), row_of(hi, 1, j))
        edge = jnp.where(row2 == 6, row_of(lo, 0, j), edge)
        edge = jnp.where(row2 == 7, row_of(lo, 1, j), edge)
        sig_out.append(edge[None])
        step_in.append(courant / (1.0 + sig[j]))
        step_out.append(courant / (1.0 + sig_out[j]))

    state = [[own_rows(u_ref, v, j) for v in range(nvar)] for j in range(3)]
    source = [[own_rows(src_ref, v, j) for v in range(nvar)] for j in range(2)]
    first, first_out = [], []
    for j in range(2):
        acc, acc_out = [None] * nvar, [None] * nvar
        for w in range(nvar):
            u = state[j][w]
            up, down = pltpu.roll(u, 7, 1), pltpu.roll(u, 1, 1)
            tp, tm = jnp.where(row == 7, 0.0, up), jnp.where(row == 0, 0.0, down)
            tp_out, tm_out = jnp.where(row == 7, up, 0.0), jnp.where(row == 0, down, 0.0)
            rm, rp = shift_r(u)
            inner = state[j + 1][w]
            if j == 0:
                dx_, nx = inner, inner
            else:
                dx_, nx = inner - state[0][w], inner + state[0][w]
            dt_, dr_ = tp - tm, rp - rm
            dt_out = tp_out - tm_out
            near = (tp + tm) + nx + (rp + rm)
            part = ((sig[j] + 6.0 * viscosity) * u - viscosity * near) + (turn(u) - source[j][w])
            for v in range(nvar):
                flux = table[v][w] * dt_ + axial[v][w] * dx_ + radial[v][w] * dr_
                flux_out = outer[v][w] * dt_out
                if v == w:
                    flux = flux + part
                    flux_out = flux_out - viscosity * (tp_out + tm_out)
                acc[v] = flux if acc[v] is None else acc[v] + flux
                acc_out[v] = flux_out if acc_out[v] is None else acc_out[v] + flux_out
        first.append([state[j][v] - (0.5 * step_in[j]) * acc[v] for v in range(nvar)])
        first_out.append([-(0.5 * step_out[j]) * acc_out[v] for v in range(nvar)])

    zero = jnp.zeros(shape, jnp.float32)
    base, total, total_out, mean, mean_out = zero, zero, zero, zero, zero
    for w in range(nvar):
        f, g = first[0][w], first_out[0][w]
        fd, fu, gd, gu = pltpu.roll(f, 1, 1), pltpu.roll(f, 7, 1), pltpu.roll(g, 1, 1), pltpu.roll(g, 7, 1)
        lt = sum(weight[v] * table[v][w] for v in range(nvar))
        lt_out = sum(weight[v] * outer[v][w] for v in range(nvar))
        lx = sum(weight[v] * axial[v][w] for v in range(nvar))
        lr = sum(weight[v] * radial[v][w] for v in range(nvar))
        for inside in (True, False):
            here, beside = (f, first[1][w]) if inside else (g, first_out[1][w])
            if inside:
                tm, tp = jnp.where(row == 0, gd, fd), jnp.where(row == 7, gu, fu)
            else:
                tm, tp = jnp.where(row == 0, fd, gd), jnp.where(row == 7, fu, gu)
            rm, rp = shift_r(here)
            near = (tp + tm) + beside + (rp + rm)
            term = (lt if inside else lt_out) * (tp - tm) + lx * beside + lr * (rp - rm)
            s = (sig if inside else sig_out)[0] + 6.0 * viscosity
            if inside:
                total = total + term + weight[w] * ((s * here - viscosity * near) - source[0][w])
                mean = mean + weight[w] * here
                base = base + weight[w] * state[0][w]
            else:
                total_out = total_out + term + weight[w] * (s * here - viscosity * near)
                mean_out = mean_out + weight[w] * here
    values = base - step_in[0] * (total + turn(mean))
    values_out = -step_out[0] * (total_out + turn(mean_out))
    values = jnp.stack([values, values_out], axis=1).reshape(nhp * 16, nr)
    nt = (((1,), (1,)), ((), ()))
    grouped = lax.dot_general(values, wave_ref[...], nt, precision=highest, preferred_element_type=jnp.float32)
    for h in range(nharm):
        mine = plane[h : h + 1, :] == last
        both = jnp.dot(
            grouped[32 * h : 32 * h + 32], pick_ref[h], precision=highest, preferred_element_type=jnp.float32
        )
        re, im = both[:16], both[16:]
        cos, sin = cos_ref[h], sin_ref[h]
        part_re = scale * jnp.sum(re * cos + im * sin, axis=0, keepdims=True)
        part_im = scale * jnp.sum(im * cos - re * sin, axis=0, keepdims=True)
        part_re, part_im = jnp.where(mine, part_re, 0.0), jnp.where(mine, part_im, 0.0)
        part_ref[:, 2 * h] = jnp.broadcast_to(part_re, (tdevices, nmode))
        part_ref[:, 2 * h + 1] = jnp.broadcast_to(part_im, (tdevices, nmode))
    part_ref[:, nhp:] = jnp.zeros((tdevices, 8 - nhp, nmode), jnp.float32)


def plane_kernel(
    tdevices,
    xdevices,
    place,
    stagger,
    a_theta,
    a_axial,
    a_radial,
    l_rows,
    u_ref,
    src_ref,
    sig_ref,
    te,
    to,
    plane,
    cos_ref,
    sin_ref,
    wave_ref,
    pick_ref,
    after,
    after2,
    after3,
    part_ref,
):
    nhp = u_ref.shape[0]
    last = (place[1] == xdevices - 1).astype(jnp.int32)
    holds = jnp.logical_or(place[1] == 0, place[1] == xdevices - 1)
    todd = lax.rem(place[0], 2) == 1

    def lo(i, rows):
        return jnp.where(todd, te[nhp, i, rows, :], to[nhp, i, rows, :])

    def hi(i, rows):
        return jnp.where(todd, to[nhp, i, rows, :], te[nhp, i, rows, :])

    @pl.when(holds)
    def _():
        refs = (plane, cos_ref, sin_ref, wave_ref, pick_ref, part_ref)
        plane_part(
            last, tdevices, stagger, a_theta, a_axial, a_radial, l_rows, u_ref, src_ref, sig_ref, lo, hi, refs
        )

    @pl.when(jnp.logical_not(holds))
    def _():
        part_ref[...] = jnp.zeros(part_ref.shape, jnp.float32)


def share_kernel(xdevices, got_ref, amp_ref):
    amp = jnp.sum(got_ref[...], axis=0)
    for d in range(xdevices):
        amp_ref[d] = amp


def finish_kernel(got_ref, plane, out_ref):
    amp = jnp.sum(got_ref[...], axis=0)
    for h in range(plane.shape[0]):
        for b in range(2):
            out_ref[h, b] = jnp.where(plane[h : h + 1, :] == b, amp[2 * h : 2 * h + 2], 0.0)


def correct_kernel(
    tdevices,
    xdevices,
    place,
    r_cols,
    got_ref,
    gust,
    second_ref,
    plane,
    cos_ref,
    sin_ref,
    wave_ref,
    pick_ref,
    out_ref,
):
    nhp, nvar, rows, nr = out_ref.shape
    nharm, nmode = plane.shape
    scale = 1.0 / math.sqrt(8 * tdevices * nr)
    last = (place[1] == xdevices - 1).astype(jnp.int32)
    holds = jnp.logical_or(place[1] == 0, place[1] == xdevices - 1)
    out_ref[...] = second_ref[...]

    @pl.when(holds)
    def _():
        amp = jnp.sum(got_ref[...], axis=0)
        for h in range(nharm):
            cos, sin = cos_ref[h, 0:8], sin_ref[h, 0:8]
            mine = plane[h : h + 1, :] == last
            miss_re = jnp.where(mine, amp[2 * h : 2 * h + 1] - gust[h, 0:1, :], 0.0)
            miss_im = jnp.where(mine, amp[2 * h + 1 : 2 * h + 2] - gust[h, 1:2, :], 0.0)
            coef = jnp.concatenate([miss_re * cos - miss_im * sin, miss_re * sin + miss_im * cos], axis=0)
            nt = (((1,), (1,)), ((), ()))
            grouped = lax.dot_general(coef, pick_ref[h], nt, precision=highest, preferred_element_type=jnp.float32)
            q = scale * jnp.dot(grouped, wave_ref[...], precision=highest, preferred_element_type=jnp.float32)
            for p in range(2):
                for v in range(nvar):
                    at = pl.ds(last * 7, 8, stride=8)
                    out_ref[2 * h + p, v, at, :] = (
                        second_ref[2 * h + p, v, at, :] - r_cols[last, v] * q[p * 8 : (p + 1) * 8]
                    )


def call(kernel, name, scalars, arrays, outs, unread=0):
    single = not isinstance(outs, (list, tuple))
    out = pl.pallas_call(
        kernel,
        in_specs=[spec(SM)] * len(scalars)
        + [spec(VM)] * (len(arrays) - unread)
        + [spec(pl.ANY)] * unread,
        out_specs=spec(VM) if single else [spec(VM)] * len(outs),
        out_shape=outs,
        compiler_params=params(name),
        name=name,
    )(*scalars, *arrays)
    return out


def local(
    state, source, sigma, stagger, a_theta, a_axial, a_radial, mode_order, mode_radial, mode_plane, gust, l_rows, r_cols
):
    nharm, two, nvar, ctheta, caxial, nradial = state.shape
    nhp, nmode = nharm * two, mode_order.shape[1]
    tdev, xdev = lax.axis_size("theta"), lax.axis_size("xr")
    nrad = 8
    block = (nhp, nvar, ctheta * caxial, nradial)
    u = state.reshape(block)
    src = source.reshape(block)
    sig = sigma.reshape(ctheta * caxial, nradial)
    place = jnp.stack([lax.axis_index("theta"), lax.axis_index("xr")]).astype(jnp.int32)

    def array(*shape):
        return jax.ShapeDtypeStruct(shape, jnp.float32)

    face = array(nhp, nvar, 8, nradial)
    packed = array(nhp + 1, nvar, 8, nradial)
    whole = array(*block)

    even_t = [(i, i ^ 1) for i in range(tdev)]
    odd_t = [(i, (i + 1) % tdev if i % 2 else (i - 1) % tdev) for i in range(tdev)]
    even_x = [(i, i ^ 1) for i in range(xdev)]
    odd_x = [(i, i + 1 if i % 2 else i - 1) for i in range(1, xdev - 1)]

    def swap(te, to, xe, xo):
        return (
            lax.ppermute(te, "theta", even_t),
            lax.ppermute(to, "theta", odd_t),
            lax.ppermute(xe, "xr", even_x),
            lax.ppermute(xo, "xr", odd_x),
        )

    coefs = (place, stagger, a_theta, a_axial, a_radial)
    faces = call(pack_kernel, "pack_faces", (place, stagger), (u, sig), [packed] * 2 + [face] * 2)
    faces = swap(*faces)
    tabs = call(
        functools.partial(table_kernel, tdev),
        "mode_tables",
        (place,),
        (mode_order, mode_radial),
        [array(nharm, 16, nmode)] * 2 + [array(nrad, nradial), array(nharm, nrad, nmode)],
    )

    def planes(after):
        return call(
            functools.partial(plane_kernel, tdev, xdev),
            "plane_part",
            (*coefs, l_rows),
            (u, src, sig, faces[0], faces[1], mode_plane, *tabs, after, faces[2], faces[3]),
            array(tdev, 8, nmode),
            3,
        )

    def first_step(after):
        return call(first_kernel, "first_step", coefs, (u, src, sig, *faces, after), [whole] + [face] * 4, 1)

    if planes_first:
        part = planes(sigma)
        first, *faces2 = first_step(part)
    else:
        first, *faces2 = first_step(sigma)
        part = planes(first)
    got = lax.all_to_all(part, "theta", 0, 0, tiled=True)
    faces2 = swap(*faces2)
    second = call(second_kernel, "second_step", coefs, (first, u, src, sig, *faces2), whole)
    amp = call(functools.partial(share_kernel, xdev), "share_amplitudes", (), (got,), array(xdev, 8, nmode))
    amp = lax.all_to_all(amp, "xr", 0, 0, tiled=True)
    fields = call(
        functools.partial(correct_kernel, tdev, xdev),
        "correct_planes",
        (place, r_cols),
        (got, gust, second, mode_plane, *tabs),
        whole,
    )
    amplitudes = call(finish_kernel, "finish_amplitudes", (), (amp, mode_plane), array(nharm, 2, two, nmode))
    return fields.reshape(state.shape), amplitudes


def solution(mesh):
    placed = (
        P(None, None, None, "theta", "xr", None),
        P(None, None, None, "theta", "xr", None),
        P("theta", "xr", None),
        P("theta"),
        P(),
        P(),
        P(),
        P(),
        P(),
        P(),
        P(),
        P(),
        P(),
    )
    return jax.shard_map(
        local,
        mesh=mesh,
        in_specs=placed,
        out_specs=(P(None, None, None, "theta", "xr", None), P()),
        check_vma=False,
    )
```

```python
import functools
import math

import jax
import jax.numpy as jnp
from jax import lax
from jax.experimental import pallas as pl
from jax.experimental.pallas import tpu as pltpu
from jax.sharding import PartitionSpec as P

courant = 0.5
viscosity = 0.1
base_frequency = 0.5
highest = lax.Precision.HIGHEST
VM = pltpu.VMEM
SM = pltpu.SMEM
planes_first = True
wide = ("pack_faces", "plane_part", "mode_tables", "first_step", "second_step")


def where():
    return lax.axis_index("theta"), lax.axis_index("xr")


def spec(space):
    return pl.BlockSpec(memory_space=space)


def params(name):
    size = 60 if name in wide else 16
    return pltpu.CompilerParams(vmem_limit_bytes=size * 1024 * 1024)


def write_faces(place, u_ref, te_ref, to_ref, xe_ref, xo_ref):
    nhp, nvar = u_ref.shape[0], u_ref.shape[1]
    todd = lax.rem(place[0], 2)
    xodd = lax.rem(place[1], 2)
    for out_ref, layer in ((te_ref, 1 - todd), (to_ref, todd)):
        start = pl.multiple_of(layer * 56, 8)
        out_ref[0:nhp] = u_ref[:, :, pl.ds(start, 8), :]
    for out_ref, row in ((xe_ref, 1 - xodd), (xo_ref, xodd)):
        for i in range(nhp):
            for v in range(nvar):
                out_ref[i, v] = u_ref[i, v, pl.ds(row * 7, 8, stride=8), :]


def pack_kernel(stagger, u_ref, sig_ref, te_ref, to_ref, xe_ref, xo_ref):
    place = where()
    write_faces(place, u_ref, te_ref, to_ref, xe_ref, xo_ref)
    nhp = u_ref.shape[0]
    nr = u_ref.shape[3]
    npass = stagger.shape[0]
    todd = lax.rem(place[0], 2)
    for out_ref, layer in ((te_ref, 1 - todd), (to_ref, todd)):
        start = pl.multiple_of(layer * 48, 8)
        out_ref[nhp, 0] = sig_ref[pl.ds(start, 8), :]
        out_ref[nhp, 1] = sig_ref[pl.ds(start + 8, 8), :]
        setting = stagger[layer * (npass - 1)].astype(jnp.float32)
        for i in range(2, out_ref.shape[1]):
            out_ref[nhp, i] = jnp.full((8, nr), setting, jnp.float32)


def step(factor, place, stagger, a_theta, a_axial, a_radial, u_ref, base_ref, src_ref, sig_ref, te, to, xe, xo, out_ref):
    nhp, nvar, rows, nr = u_ref.shape
    tcells = rows // 8
    cpp = tcells // stagger.shape[0]
    todd = lax.rem(place[0], 2) == 1
    xodd = lax.rem(place[1], 2) == 1
    shape = (nhp, 8, nr)
    row = lax.broadcasted_iota(jnp.int32, shape, 1)
    lane = lax.broadcasted_iota(jnp.int32, shape, 2)
    axial = [[0.5 * a_axial[v, w] for w in range(nvar)] for v in range(nvar)]
    radial = [[0.5 * a_radial[v, w] for w in range(nvar)] for v in range(nvar)]
    for t in range(tcells):
        setting = stagger[t // cpp]
        tile = slice(8 * t, 8 * t + 8)
        sig = sig_ref[tile, :][None]
        own = sig + 6.0 * viscosity
        scaled = (factor * courant) / (1.0 + sig)
        acc = [None] * nvar
        for w in range(nvar):
            u = u_ref[:, w, tile, :]
            if t == 0:
                tm = jnp.where(todd, te[0:nhp, w], to[0:nhp, w])
            else:
                tm = u_ref[:, w, 8 * t - 8 : 8 * t, :]
            if t == tcells - 1:
                tp = jnp.where(todd, to[0:nhp, w], te[0:nhp, w])
            else:
                tp = u_ref[:, w, 8 * t + 8 : 8 * t + 16, :]
            e = xe[:, w, t : t + 1, :]
            o = xo[:, w, t : t + 1, :]
            xlo = jnp.where(xodd, e, o)
            xhi = jnp.where(xodd, o, e)
            xm = jnp.where(row == 0, jnp.broadcast_to(xlo, shape), pltpu.roll(u, 1, 1))
            xp = jnp.where(row == 7, jnp.broadcast_to(xhi, shape), pltpu.roll(u, 7, 1))
            rm = jnp.where(lane == 0, 0.0, pltpu.roll(u, 1, 2))
            rp = jnp.where(lane == nr - 1, 0.0, pltpu.roll(u, nr - 1, 2))
            dt_, dx_, dr_ = tp - tm, xp - xm, rp - rm
            near = ((tp + tm) + (xp + xm)) + (rp + rm)
            turned = []
            for h in range(nhp // 2):
                freq = base_frequency * (1.0 + h)
                turned.append(-freq * u[2 * h + 1 : 2 * h + 2])
                turned.append(freq * u[2 * h : 2 * h + 1])
            local_part = (own * u - viscosity * near) + (jnp.concatenate(turned, axis=0) - src_ref[:, w, tile, :])
            for v in range(nvar):
                flux = (0.5 * a_theta[setting, v, w]) * dt_ + axial[v][w] * dx_ + radial[v][w] * dr_
                if v == w:
                    flux = flux + local_part
                acc[v] = flux if acc[v] is None else acc[v] + flux
        for v in range(nvar):
            out_ref[:, v, tile, :] = base_ref[:, v, tile, :] - scaled * acc[v]


def first_kernel(stagger, a_theta, a_axial, a_radial, u_ref, src_ref, sig_ref, te, to, xe, xo, after, out_ref, te2, to2, xe2, xo2
):
    place = where()
    step(0.5, place, stagger, a_theta, a_axial, a_radial, u_ref, u_ref, src_ref, sig_ref, te, to, xe, xo, out_ref)
    write_faces(place, out_ref, te2, to2, xe2, xo2)


def table_kernel(tdevices, order, radial, cos_ref, sin_ref, wave_ref, pick_ref):
    place = where()
    nharm, nmode = order.shape
    tcells = 8
    total = tcells * tdevices
    row = lax.broadcasted_iota(jnp.int32, (2 * tcells, nmode), 0)
    cell = place[0] * tcells + jnp.where(row < 12, row, row - 16)
    nrad, nr = wave_ref.shape
    wave_ref[...] = radial_table(nrad, nr)
    for h in range(nharm):
        turns = lax.rem(order[h : h + 1, :] * cell + 64 * total, total)
        angle = 2.0 * math.pi * turns.astype(jnp.float32) / total
        cos_ref[h] = jnp.cos(angle)
        sin_ref[h] = jnp.sin(angle)
        n = lax.broadcasted_iota(jnp.int32, (nrad, nmode), 0)
        pick_ref[h] = (n == radial[h : h + 1, :]).astype(jnp.float32)


def radial_table(nrad, nr):
    n = lax.broadcasted_iota(jnp.int32, (nrad, nr), 0)
    pos = lax.broadcasted_iota(jnp.int32, (nrad, nr), 1).astype(jnp.float32) + 0.5
    wave = math.sqrt(2.0) * jnp.cos(math.pi * n.astype(jnp.float32) * pos / nr)
    return jnp.where(n == 0, 1.0, wave)


def turn(u):
    out = []
    for h in range(u.shape[0] // 2):
        freq = base_frequency * (1.0 + h)
        out.append(-freq * u[2 * h + 1 : 2 * h + 2])
        out.append(freq * u[2 * h : 2 * h + 1])
    return jnp.concatenate(out, axis=0)


def plane_part(last, tdevices, stagger, a_theta, a_axial, a_radial, l_rows, u_ref, src_ref, sig_ref, lo, hi, refs):
    plane, cos_ref, sin_ref, wave_ref, pick_ref, part_ref = refs
    nhp, nvar, rows, nr = u_ref.shape
    nharm, nmode = plane.shape
    nset = a_theta.shape[0]
    scale = 1.0 / math.sqrt(8 * tdevices * nr)
    shape = (nhp, 8, nr)
    row = lax.broadcasted_iota(jnp.int32, shape, 1)
    lane = lax.broadcasted_iota(jnp.int32, shape, 2)
    row1, row2 = row[0], lax.broadcasted_iota(jnp.int32, (8, nr), 0)
    side = (1 - 2 * last).astype(jnp.float32)
    at = [last * 7 + j * (1 - 2 * last) for j in range(3)]

    def own_rows(ref, v, j):
        return jnp.stack([ref[i, v, pl.ds(at[j], 8, stride=8), :] for i in range(nhp)])

    def shift_r(u):
        return (
            jnp.where(lane == 0, 0.0, pltpu.roll(u, 1, 2)),
            jnp.where(lane == nr - 1, 0.0, pltpu.roll(u, nr - 1, 2)),
        )

    def row_of(face, i, j):
        return jnp.broadcast_to(face(i, pl.ds(at[j], 1)), (8, nr))

    settings = jnp.where(row2 < 4, hi(2, slice(0, 8)), lo(2, slice(0, 8)))
    table = [[None] * nvar for _ in range(nvar)]
    outer = [[None] * nvar for _ in range(nvar)]
    for v in range(nvar):
        for w in range(nvar):
            table[v][w] = jnp.where(row2 < 4, 0.5 * a_theta[stagger[0], v, w], 0.5 * a_theta[stagger[1], v, w])[None]
            value = jnp.full((8, nr), 0.5 * a_theta[nset - 1, v, w], jnp.float32)
            for s in range(nset - 1):
                value = jnp.where(settings == float(s), 0.5 * a_theta[s, v, w], value)
            outer[v][w] = value[None]
    axial = [[0.5 * side * a_axial[v, w] for w in range(nvar)] for v in range(nvar)]
    radial = [[0.5 * a_radial[v, w] for w in range(nvar)] for v in range(nvar)]
    weight = [l_rows[last, v] for v in range(nvar)]

    sig, sig_out, step_in, step_out = [], [], [], []
    for j in range(2):
        sig.append(sig_ref[pl.ds(at[j], 8, stride=8), :][None])
        edge = jnp.where(row2 == 0, row_of(hi, 0, j), row_of(hi, 1, j))
        edge = jnp.where(row2 == 6, row_of(lo, 0, j), edge)
        edge = jnp.where(row2 == 7, row_of(lo, 1, j), edge)
        sig_out.append(edge[None])
        step_in.append(courant / (1.0 + sig[j]))
        step_out.append(courant / (1.0 + sig_out[j]))

    state = [[own_rows(u_ref, v, j) for v in range(nvar)] for j in range(3)]
    source = [[own_rows(src_ref, v, j) for v in range(nvar)] for j in range(2)]
    first, first_out = [], []
    for j in range(2):
        acc, acc_out = [None] * nvar, [None] * nvar
        for w in range(nvar):
            u = state[j][w]
            up, down = pltpu.roll(u, 7, 1), pltpu.roll(u, 1, 1)
            tp, tm = jnp.where(row == 7, 0.0, up), jnp.where(row == 0, 0.0, down)
            tp_out, tm_out = jnp.where(row == 7, up, 0.0), jnp.where(row == 0, down, 0.0)
            rm, rp = shift_r(u)
            inner = state[j + 1][w]
            if j == 0:
                dx_, nx = inner, inner
            else:
                dx_, nx = inner - state[0][w], inner + state[0][w]
            dt_, dr_ = tp - tm, rp - rm
            dt_out = tp_out - tm_out
            near = (tp + tm) + nx + (rp + rm)
            part = ((sig[j] + 6.0 * viscosity) * u - viscosity * near) + (turn(u) - source[j][w])
            for v in range(nvar):
                flux = table[v][w] * dt_ + axial[v][w] * dx_ + radial[v][w] * dr_
                flux_out = outer[v][w] * dt_out
                if v == w:
                    flux = flux + part
                    flux_out = flux_out - viscosity * (tp_out + tm_out)
                acc[v] = flux if acc[v] is None else acc[v] + flux
                acc_out[v] = flux_out if acc_out[v] is None else acc_out[v] + flux_out
        first.append([state[j][v] - (0.5 * step_in[j]) * acc[v] for v in range(nvar)])
        first_out.append([-(0.5 * step_out[j]) * acc_out[v] for v in range(nvar)])

    zero = jnp.zeros(shape, jnp.float32)
    base, total, total_out, mean, mean_out = zero, zero, zero, zero, zero
    for w in range(nvar):
        f, g = first[0][w], first_out[0][w]
        fd, fu, gd, gu = pltpu.roll(f, 1, 1), pltpu.roll(f, 7, 1), pltpu.roll(g, 1, 1), pltpu.roll(g, 7, 1)
        lt = sum(weight[v] * table[v][w] for v in range(nvar))
        lt_out = sum(weight[v] * outer[v][w] for v in range(nvar))
        lx = sum(weight[v] * axial[v][w] for v in range(nvar))
        lr = sum(weight[v] * radial[v][w] for v in range(nvar))
        for inside in (True, False):
            here, beside = (f, first[1][w]) if inside else (g, first_out[1][w])
            if inside:
                tm, tp = jnp.where(row == 0, gd, fd), jnp.where(row == 7, gu, fu)
            else:
                tm, tp = jnp.where(row == 0, fd, gd), jnp.where(row == 7, fu, gu)
            rm, rp = shift_r(here)
            near = (tp + tm) + beside + (rp + rm)
            term = (lt if inside else lt_out) * (tp - tm) + lx * beside + lr * (rp - rm)
            s = (sig if inside else sig_out)[0] + 6.0 * viscosity
            if inside:
                total = total + term + weight[w] * ((s * here - viscosity * near) - source[0][w])
                mean = mean + weight[w] * here
                base = base + weight[w] * state[0][w]
            else:
                total_out = total_out + term + weight[w] * (s * here - viscosity * near)
                mean_out = mean_out + weight[w] * here
    values = base - step_in[0] * (total + turn(mean))
    values_out = -step_out[0] * (total_out + turn(mean_out))
    values = jnp.stack([values, values_out], axis=1).reshape(nhp * 16, nr)
    nt = (((1,), (1,)), ((), ()))
    grouped = lax.dot_general(values, wave_ref[...], nt, precision=highest, preferred_element_type=jnp.float32)
    for h in range(nharm):
        mine = plane[h : h + 1, :] == last
        both = jnp.dot(
            grouped[32 * h : 32 * h + 32], pick_ref[h], precision=highest, preferred_element_type=jnp.float32
        )
        re, im = both[:16], both[16:]
        cos, sin = cos_ref[h], sin_ref[h]
        part_re = scale * jnp.sum(re * cos + im * sin, axis=0, keepdims=True)
        part_im = scale * jnp.sum(im * cos - re * sin, axis=0, keepdims=True)
        part_re, part_im = jnp.where(mine, part_re, 0.0), jnp.where(mine, part_im, 0.0)
        part_ref[:, 2 * h] = jnp.broadcast_to(part_re, (tdevices, nmode))
        part_ref[:, 2 * h + 1] = jnp.broadcast_to(part_im, (tdevices, nmode))
    part_ref[:, nhp:] = jnp.zeros((tdevices, 8 - nhp, nmode), jnp.float32)


def plane_kernel(
    tdevices,
    xdevices,
    stagger,
    a_theta,
    a_axial,
    a_radial,
    l_rows,
    u_ref,
    src_ref,
    sig_ref,
    te,
    to,
    plane,
    cos_ref,
    sin_ref,
    wave_ref,
    pick_ref,
    after,
    after2,
    after3,
    part_ref,
):
    place = where()
    nhp = u_ref.shape[0]
    last = (place[1] == xdevices - 1).astype(jnp.int32)
    holds = jnp.logical_or(place[1] == 0, place[1] == xdevices - 1)
    todd = lax.rem(place[0], 2) == 1

    def lo(i, rows):
        return jnp.where(todd, te[nhp, i, rows, :], to[nhp, i, rows, :])

    def hi(i, rows):
        return jnp.where(todd, to[nhp, i, rows, :], te[nhp, i, rows, :])

    @pl.when(holds)
    def _():
        refs = (plane, cos_ref, sin_ref, wave_ref, pick_ref, part_ref)
        plane_part(
            last, tdevices, stagger, a_theta, a_axial, a_radial, l_rows, u_ref, src_ref, sig_ref, lo, hi, refs
        )

    @pl.when(jnp.logical_not(holds))
    def _():
        part_ref[...] = jnp.zeros(part_ref.shape, jnp.float32)


def share_kernel(xdevices, got_ref, amp_ref):
    amp = jnp.sum(got_ref[...], axis=0)
    for d in range(xdevices):
        amp_ref[d] = amp


def finish_kernel(got_ref, plane, out_ref):
    amp = jnp.sum(got_ref[...], axis=0)
    for h in range(plane.shape[0]):
        for b in range(2):
            out_ref[h, b] = jnp.where(plane[h : h + 1, :] == b, amp[2 * h : 2 * h + 2], 0.0)


def second_kernel(
    tdevices,
    xdevices,
    stagger,
    a_theta,
    a_axial,
    a_radial,
    r_cols,
    u_ref,
    base_ref,
    src_ref,
    sig_ref,
    te,
    to,
    xe,
    xo,
    got_ref,
    gust,
    plane,
    cos_ref,
    sin_ref,
    wave_ref,
    pick_ref,
    out_ref,
):
    place = where()
    step(1.0, place, stagger, a_theta, a_axial, a_radial, u_ref, base_ref, src_ref, sig_ref, te, to, xe, xo, out_ref)
    nhp, nvar, rows, nr = out_ref.shape
    nharm, nmode = plane.shape
    scale = 1.0 / math.sqrt(8 * tdevices * nr)
    last = (place[1] == xdevices - 1).astype(jnp.int32)
    holds = jnp.logical_or(place[1] == 0, place[1] == xdevices - 1)

    @pl.when(holds)
    def _():
        amp = jnp.sum(got_ref[...], axis=0)
        for h in range(nharm):
            cos, sin = cos_ref[h, 0:8], sin_ref[h, 0:8]
            mine = plane[h : h + 1, :] == last
            miss_re = jnp.where(mine, amp[2 * h : 2 * h + 1] - gust[h, 0:1, :], 0.0)
            miss_im = jnp.where(mine, amp[2 * h + 1 : 2 * h + 2] - gust[h, 1:2, :], 0.0)
            coef = jnp.concatenate([miss_re * cos - miss_im * sin, miss_re * sin + miss_im * cos], axis=0)
            nt = (((1,), (1,)), ((), ()))
            grouped = lax.dot_general(coef, pick_ref[h], nt, precision=highest, preferred_element_type=jnp.float32)
            q = scale * jnp.dot(grouped, wave_ref[...], precision=highest, preferred_element_type=jnp.float32)
            for p in range(2):
                for v in range(nvar):
                    at = pl.ds(last * 7, 8, stride=8)
                    out_ref[2 * h + p, v, at, :] = (
                        out_ref[2 * h + p, v, at, :] - r_cols[last, v] * q[p * 8 : (p + 1) * 8]
                    )


def call(kernel, name, scalars, arrays, outs, unread=0):
    single = not isinstance(outs, (list, tuple))
    out = pl.pallas_call(
        kernel,
        in_specs=[spec(SM)] * len(scalars)
        + [spec(VM)] * (len(arrays) - unread)
        + [spec(pl.ANY)] * unread,
        out_specs=spec(VM) if single else [spec(VM)] * len(outs),
        out_shape=outs,
        compiler_params=params(name),
        name=name,
    )(*scalars, *arrays)
    return out


def local(
    state, source, sigma, stagger, a_theta, a_axial, a_radial, mode_order, mode_radial, mode_plane, gust, l_rows, r_cols
):
    nharm, two, nvar, ctheta, caxial, nradial = state.shape
    nhp, nmode = nharm * two, mode_order.shape[1]
    tdev, xdev = lax.axis_size("theta"), lax.axis_size("xr")
    nrad = 8
    block = (nhp, nvar, ctheta * caxial, nradial)
    u = state.reshape(block)
    src = source.reshape(block)
    sig = sigma.reshape(ctheta * caxial, nradial)

    def array(*shape):
        return jax.ShapeDtypeStruct(shape, jnp.float32)

    face = array(nhp, nvar, 8, nradial)
    packed = array(nhp + 1, nvar, 8, nradial)
    whole = array(*block)

    even_t = [(i, i ^ 1) for i in range(tdev)]
    odd_t = [(i, (i + 1) % tdev if i % 2 else (i - 1) % tdev) for i in range(tdev)]
    even_x = [(i, i ^ 1) for i in range(xdev)]
    odd_x = [(i, i + 1 if i % 2 else i - 1) for i in range(1, xdev - 1)]

    def swap(te, to, xe, xo):
        return (
            lax.ppermute(te, "theta", even_t),
            lax.ppermute(to, "theta", odd_t),
            lax.ppermute(xe, "xr", even_x),
            lax.ppermute(xo, "xr", odd_x),
        )

    coefs = (stagger, a_theta, a_axial, a_radial)
    faces = call(pack_kernel, "pack_faces", (stagger,), (u, sig), [packed] * 2 + [face] * 2)
    faces = swap(*faces)
    tabs = call(
        functools.partial(table_kernel, tdev),
        "mode_tables",
        (),
        (mode_order, mode_radial),
        [array(nharm, 16, nmode)] * 2 + [array(nrad, nradial), array(nharm, nrad, nmode)],
    )

    def planes(after):
        return call(
            functools.partial(plane_kernel, tdev, xdev),
            "plane_part",
            (*coefs, l_rows),
            (u, src, sig, faces[0], faces[1], mode_plane, *tabs, after, faces[2], faces[3]),
            array(tdev, 8, nmode),
            3,
        )

    def first_step(after):
        return call(first_kernel, "first_step", coefs, (u, src, sig, *faces, after), [whole] + [face] * 4, 1)

    if planes_first:
        part = planes(sigma)
        first, *faces2 = first_step(part)
    else:
        first, *faces2 = first_step(sigma)
        part = planes(first)
    got = lax.all_to_all(part, "theta", 0, 0, tiled=True)
    faces2 = swap(*faces2)
    amp = call(functools.partial(share_kernel, xdev), "share_amplitudes", (), (got,), array(xdev, 8, nmode))
    amp = lax.all_to_all(amp, "xr", 0, 0, tiled=True)
    fields = call(
        functools.partial(second_kernel, tdev, xdev),
        "second_step",
        (*coefs, r_cols),
        (first, u, src, sig, *faces2, got, gust, mode_plane, *tabs),
        whole,
    )
    amplitudes = call(finish_kernel, "finish_amplitudes", (), (amp, mode_plane), array(nharm, 2, two, nmode))
    return fields.reshape(state.shape), amplitudes


def solution(mesh):
    placed = (
        P(None, None, None, "theta", "xr", None),
        P(None, None, None, "theta", "xr", None),
        P("theta", "xr", None),
        P("theta"),
        P(),
        P(),
        P(),
        P(),
        P(),
        P(),
        P(),
        P(),
        P(),
    )
    return jax.shard_map(
        local,
        mesh=mesh,
        in_specs=placed,
        out_specs=(P(None, None, None, "theta", "xr", None), P()),
        check_vma=False,
    )
```

```python
import functools
import math

import jax
import jax.numpy as jnp
from jax import lax
from jax.experimental import pallas as pl
from jax.experimental.pallas import tpu as pltpu
from jax.sharding import PartitionSpec as P

courant = 0.5
viscosity = 0.1
base_frequency = 0.5
highest = lax.Precision.HIGHEST
VM = pltpu.VMEM
SM = pltpu.SMEM
planes_first = True
wide = ("pack_faces", "plane_part", "mode_tables", "first_step", "second_step")


def where():
    return lax.axis_index("theta"), lax.axis_index("xr")


def spec(space):
    return pl.BlockSpec(memory_space=space)


def params(name):
    size = 60 if name in wide else 16
    return pltpu.CompilerParams(vmem_limit_bytes=size * 1024 * 1024)


def write_faces(place, u_ref, te_ref, to_ref, xe_ref, xo_ref):
    nhp, nvar = u_ref.shape[0], u_ref.shape[1]
    todd = lax.rem(place[0], 2)
    xodd = lax.rem(place[1], 2)
    for out_ref, layer in ((te_ref, 1 - todd), (to_ref, todd)):
        start = pl.multiple_of(layer * 56, 8)
        out_ref[0:nhp] = u_ref[:, :, pl.ds(start, 8), :]
    for out_ref, row in ((xe_ref, 1 - xodd), (xo_ref, xodd)):
        for i in range(nhp):
            for v in range(nvar):
                out_ref[i, v] = u_ref[i, v, pl.ds(row * 7, 8, stride=8), :]


def pack_kernel(stagger, u_ref, sig_ref, te_ref, to_ref, xe_ref, xo_ref):
    place = where()
    write_faces(place, u_ref, te_ref, to_ref, xe_ref, xo_ref)
    nhp = u_ref.shape[0]
    nr = u_ref.shape[3]
    npass = stagger.shape[0]
    todd = lax.rem(place[0], 2)
    for out_ref, layer in ((te_ref, 1 - todd), (to_ref, todd)):
        start = pl.multiple_of(layer * 48, 8)
        out_ref[nhp, 0] = sig_ref[pl.ds(start, 8), :]
        out_ref[nhp, 1] = sig_ref[pl.ds(start + 8, 8), :]
        setting = stagger[layer * (npass - 1)].astype(jnp.float32)
        for i in range(2, out_ref.shape[1]):
            out_ref[nhp, i] = jnp.full((8, nr), setting, jnp.float32)


def step(factor, place, stagger, a_theta, a_axial, a_radial, u_ref, base_ref, src_ref, sig_ref, te, to, xe, xo, out_ref):
    nhp, nvar, rows, nr = u_ref.shape
    tcells = rows // 8
    cpp = tcells // stagger.shape[0]
    todd = lax.rem(place[0], 2) == 1
    xodd = lax.rem(place[1], 2) == 1
    shape = (nhp, 8, nr)
    row = lax.broadcasted_iota(jnp.int32, shape, 1)
    lane = lax.broadcasted_iota(jnp.int32, shape, 2)
    axial = [[0.5 * a_axial[v, w] for w in range(nvar)] for v in range(nvar)]
    radial = [[0.5 * a_radial[v, w] for w in range(nvar)] for v in range(nvar)]
    for t in range(tcells):
        setting = stagger[t // cpp]
        tile = slice(8 * t, 8 * t + 8)
        sig = sig_ref[tile, :][None]
        own = sig + 6.0 * viscosity
        scaled = (factor * courant) / (1.0 + sig)
        acc = [None] * nvar
        for w in range(nvar):
            u = u_ref[:, w, tile, :]
            if t == 0:
                tm = jnp.where(todd, te[0:nhp, w], to[0:nhp, w])
            else:
                tm = u_ref[:, w, 8 * t - 8 : 8 * t, :]
            if t == tcells - 1:
                tp = jnp.where(todd, to[0:nhp, w], te[0:nhp, w])
            else:
                tp = u_ref[:, w, 8 * t + 8 : 8 * t + 16, :]
            e = xe[:, w, t : t + 1, :]
            o = xo[:, w, t : t + 1, :]
            xlo = jnp.where(xodd, e, o)
            xhi = jnp.where(xodd, o, e)
            xm = jnp.where(row == 0, jnp.broadcast_to(xlo, shape), pltpu.roll(u, 1, 1))
            xp = jnp.where(row == 7, jnp.broadcast_to(xhi, shape), pltpu.roll(u, 7, 1))
            rm = jnp.where(lane == 0, 0.0, pltpu.roll(u, 1, 2))
            rp = jnp.where(lane == nr - 1, 0.0, pltpu.roll(u, nr - 1, 2))
            dt_, dx_, dr_ = tp - tm, xp - xm, rp - rm
            near = ((tp + tm) + (xp + xm)) + (rp + rm)
            turned = []
            for h in range(nhp // 2):
                freq = base_frequency * (1.0 + h)
                turned.append(-freq * u[2 * h + 1 : 2 * h + 2])
                turned.append(freq * u[2 * h : 2 * h + 1])
            local_part = (own * u - viscosity * near) + (jnp.concatenate(turned, axis=0) - src_ref[:, w, tile, :])
            for v in range(nvar):
                flux = (0.5 * a_theta[setting, v, w]) * dt_ + axial[v][w] * dx_ + radial[v][w] * dr_
                if v == w:
                    flux = flux + local_part
                acc[v] = flux if acc[v] is None else acc[v] + flux
        for v in range(nvar):
            out_ref[:, v, tile, :] = base_ref[:, v, tile, :] - scaled * acc[v]


def first_kernel(stagger, a_theta, a_axial, a_radial, u_ref, src_ref, sig_ref, te, to, xe, xo, after, out_ref, te2, to2, xe2, xo2
):
    place = where()
    step(0.5, place, stagger, a_theta, a_axial, a_radial, u_ref, u_ref, src_ref, sig_ref, te, to, xe, xo, out_ref)
    write_faces(place, out_ref, te2, to2, xe2, xo2)


def table_kernel(
    tdevices, xdevices, order, radial, u_ref, src_ref, cos_ref, sin_ref, wave_ref, pick_ref, rows_ref
):
    place = where()
    last = (place[1] == xdevices - 1).astype(jnp.int32)
    for ref, first_slot, count in ((u_ref, 0, 3), (src_ref, 3, 2)):
        for j in range(count):
            at = pl.ds(last * 7 + j * (1 - 2 * last), 8, stride=8)
            for i in range(u_ref.shape[0]):
                for v in range(u_ref.shape[1]):
                    rows_ref[first_slot + j, i, v] = ref[i, v, at, :]
    nharm, nmode = order.shape
    tcells = 8
    total = tcells * tdevices
    row = lax.broadcasted_iota(jnp.int32, (2 * tcells, nmode), 0)
    cell = place[0] * tcells + jnp.where(row < 12, row, row - 16)
    nrad, nr = wave_ref.shape
    wave_ref[...] = radial_table(nrad, nr)
    for h in range(nharm):
        turns = lax.rem(order[h : h + 1, :] * cell + 64 * total, total)
        angle = 2.0 * math.pi * turns.astype(jnp.float32) / total
        cos_ref[h] = jnp.cos(angle)
        sin_ref[h] = jnp.sin(angle)
        n = lax.broadcasted_iota(jnp.int32, (nrad, nmode), 0)
        pick_ref[h] = (n == radial[h : h + 1, :]).astype(jnp.float32)


def radial_table(nrad, nr):
    n = lax.broadcasted_iota(jnp.int32, (nrad, nr), 0)
    pos = lax.broadcasted_iota(jnp.int32, (nrad, nr), 1).astype(jnp.float32) + 0.5
    wave = math.sqrt(2.0) * jnp.cos(math.pi * n.astype(jnp.float32) * pos / nr)
    return jnp.where(n == 0, 1.0, wave)


def turn(u):
    out = []
    for h in range(u.shape[0] // 2):
        freq = base_frequency * (1.0 + h)
        out.append(-freq * u[2 * h + 1 : 2 * h + 2])
        out.append(freq * u[2 * h : 2 * h + 1])
    return jnp.concatenate(out, axis=0)


def plane_part(last, tdevices, stagger, a_theta, a_axial, a_radial, l_rows, rows_ref, sig_ref, lo, hi, refs):
    plane, cos_ref, sin_ref, wave_ref, pick_ref, part_ref = refs
    _, nhp, nvar, _, nr = rows_ref.shape
    nharm, nmode = plane.shape
    nset = a_theta.shape[0]
    scale = 1.0 / math.sqrt(8 * tdevices * nr)
    shape = (nhp, 8, nr)
    row = lax.broadcasted_iota(jnp.int32, shape, 1)
    lane = lax.broadcasted_iota(jnp.int32, shape, 2)
    row1, row2 = row[0], lax.broadcasted_iota(jnp.int32, (8, nr), 0)
    side = (1 - 2 * last).astype(jnp.float32)
    at = [last * 7 + j * (1 - 2 * last) for j in range(3)]

    def shift_r(u):
        return (
            jnp.where(lane == 0, 0.0, pltpu.roll(u, 1, 2)),
            jnp.where(lane == nr - 1, 0.0, pltpu.roll(u, nr - 1, 2)),
        )

    def row_of(face, i, j):
        return jnp.broadcast_to(face(i, pl.ds(at[j], 1)), (8, nr))

    settings = jnp.where(row2 < 4, hi(2, slice(0, 8)), lo(2, slice(0, 8)))
    table = [[None] * nvar for _ in range(nvar)]
    outer = [[None] * nvar for _ in range(nvar)]
    for v in range(nvar):
        for w in range(nvar):
            table[v][w] = jnp.where(row2 < 4, 0.5 * a_theta[stagger[0], v, w], 0.5 * a_theta[stagger[1], v, w])[None]
            value = jnp.full((8, nr), 0.5 * a_theta[nset - 1, v, w], jnp.float32)
            for s in range(nset - 1):
                value = jnp.where(settings == float(s), 0.5 * a_theta[s, v, w], value)
            outer[v][w] = value[None]
    axial = [[0.5 * side * a_axial[v, w] for w in range(nvar)] for v in range(nvar)]
    radial = [[0.5 * a_radial[v, w] for w in range(nvar)] for v in range(nvar)]
    weight = [l_rows[last, v] for v in range(nvar)]

    sig, sig_out, step_in, step_out = [], [], [], []
    for j in range(2):
        sig.append(sig_ref[pl.ds(at[j], 8, stride=8), :][None])
        edge = jnp.where(row2 == 0, row_of(hi, 0, j), row_of(hi, 1, j))
        edge = jnp.where(row2 == 6, row_of(lo, 0, j), edge)
        edge = jnp.where(row2 == 7, row_of(lo, 1, j), edge)
        sig_out.append(edge[None])
        step_in.append(courant / (1.0 + sig[j]))
        step_out.append(courant / (1.0 + sig_out[j]))

    state = [[rows_ref[j, :, v] for v in range(nvar)] for j in range(3)]
    source = [[rows_ref[3 + j, :, v] for v in range(nvar)] for j in range(2)]
    first, first_out = [], []
    for j in range(2):
        acc, acc_out = [None] * nvar, [None] * nvar
        for w in range(nvar):
            u = state[j][w]
            up, down = pltpu.roll(u, 7, 1), pltpu.roll(u, 1, 1)
            tp, tm = jnp.where(row == 7, 0.0, up), jnp.where(row == 0, 0.0, down)
            tp_out, tm_out = jnp.where(row == 7, up, 0.0), jnp.where(row == 0, down, 0.0)
            rm, rp = shift_r(u)
            inner = state[j + 1][w]
            if j == 0:
                dx_, nx = inner, inner
            else:
                dx_, nx = inner - state[0][w], inner + state[0][w]
            dt_, dr_ = tp - tm, rp - rm
            dt_out = tp_out - tm_out
            near = (tp + tm) + nx + (rp + rm)
            part = ((sig[j] + 6.0 * viscosity) * u - viscosity * near) + (turn(u) - source[j][w])
            for v in range(nvar):
                flux = table[v][w] * dt_ + axial[v][w] * dx_ + radial[v][w] * dr_
                flux_out = outer[v][w] * dt_out
                if v == w:
                    flux = flux + part
                    flux_out = flux_out - viscosity * (tp_out + tm_out)
                acc[v] = flux if acc[v] is None else acc[v] + flux
                acc_out[v] = flux_out if acc_out[v] is None else acc_out[v] + flux_out
        first.append([state[j][v] - (0.5 * step_in[j]) * acc[v] for v in range(nvar)])
        first_out.append([-(0.5 * step_out[j]) * acc_out[v] for v in range(nvar)])

    zero = jnp.zeros(shape, jnp.float32)
    base, total, total_out, mean, mean_out = zero, zero, zero, zero, zero
    for w in range(nvar):
        f, g = first[0][w], first_out[0][w]
        fd, fu, gd, gu = pltpu.roll(f, 1, 1), pltpu.roll(f, 7, 1), pltpu.roll(g, 1, 1), pltpu.roll(g, 7, 1)
        lt = sum(weight[v] * table[v][w] for v in range(nvar))
        lt_out = sum(weight[v] * outer[v][w] for v in range(nvar))
        lx = sum(weight[v] * axial[v][w] for v in range(nvar))
        lr = sum(weight[v] * radial[v][w] for v in range(nvar))
        for inside in (True, False):
            here, beside = (f, first[1][w]) if inside else (g, first_out[1][w])
            if inside:
                tm, tp = jnp.where(row == 0, gd, fd), jnp.where(row == 7, gu, fu)
            else:
                tm, tp = jnp.where(row == 0, fd, gd), jnp.where(row == 7, fu, gu)
            rm, rp = shift_r(here)
            near = (tp + tm) + beside + (rp + rm)
            term = (lt if inside else lt_out) * (tp - tm) + lx * beside + lr * (rp - rm)
            s = (sig if inside else sig_out)[0] + 6.0 * viscosity
            if inside:
                total = total + term + weight[w] * ((s * here - viscosity * near) - source[0][w])
                mean = mean + weight[w] * here
                base = base + weight[w] * state[0][w]
            else:
                total_out = total_out + term + weight[w] * (s * here - viscosity * near)
                mean_out = mean_out + weight[w] * here
    values = base - step_in[0] * (total + turn(mean))
    values_out = -step_out[0] * (total_out + turn(mean_out))
    values = jnp.stack([values, values_out], axis=1).reshape(nhp * 16, nr)
    nt = (((1,), (1,)), ((), ()))
    grouped = lax.dot_general(values, wave_ref[...], nt, precision=highest, preferred_element_type=jnp.float32)
    for h in range(nharm):
        mine = plane[h : h + 1, :] == last
        both = jnp.dot(
            grouped[32 * h : 32 * h + 32], pick_ref[h], precision=highest, preferred_element_type=jnp.float32
        )
        re, im = both[:16], both[16:]
        cos, sin = cos_ref[h], sin_ref[h]
        part_re = scale * jnp.sum(re * cos + im * sin, axis=0, keepdims=True)
        part_im = scale * jnp.sum(im * cos - re * sin, axis=0, keepdims=True)
        part_re, part_im = jnp.where(mine, part_re, 0.0), jnp.where(mine, part_im, 0.0)
        part_ref[:, 2 * h] = jnp.broadcast_to(part_re, (tdevices, nmode))
        part_ref[:, 2 * h + 1] = jnp.broadcast_to(part_im, (tdevices, nmode))
    part_ref[:, nhp:] = jnp.zeros((tdevices, 8 - nhp, nmode), jnp.float32)


def plane_kernel(
    tdevices,
    xdevices,
    stagger,
    a_theta,
    a_axial,
    a_radial,
    l_rows,
    rows_ref,
    sig_ref,
    te,
    to,
    plane,
    cos_ref,
    sin_ref,
    wave_ref,
    pick_ref,
    after,
    after2,
    after3,
    part_ref,
):
    place = where()
    nhp = rows_ref.shape[1]
    last = (place[1] == xdevices - 1).astype(jnp.int32)
    holds = jnp.logical_or(place[1] == 0, place[1] == xdevices - 1)
    todd = lax.rem(place[0], 2) == 1

    def lo(i, rows):
        return jnp.where(todd, te[nhp, i, rows, :], to[nhp, i, rows, :])

    def hi(i, rows):
        return jnp.where(todd, to[nhp, i, rows, :], te[nhp, i, rows, :])

    @pl.when(holds)
    def _():
        refs = (plane, cos_ref, sin_ref, wave_ref, pick_ref, part_ref)
        plane_part(
            last, tdevices, stagger, a_theta, a_axial, a_radial, l_rows, rows_ref, sig_ref, lo, hi, refs
        )

    @pl.when(jnp.logical_not(holds))
    def _():
        part_ref[...] = jnp.zeros(part_ref.shape, jnp.float32)


def share_kernel(xdevices, got_ref, amp_ref):
    amp = jnp.sum(got_ref[...], axis=0)
    for d in range(xdevices):
        amp_ref[d] = amp


def finish_kernel(got_ref, plane, out_ref):
    amp = jnp.sum(got_ref[...], axis=0)
    for h in range(plane.shape[0]):
        for b in range(2):
            out_ref[h, b] = jnp.where(plane[h : h + 1, :] == b, amp[2 * h : 2 * h + 2], 0.0)


def second_kernel(
    tdevices,
    xdevices,
    stagger,
    a_theta,
    a_axial,
    a_radial,
    r_cols,
    u_ref,
    base_ref,
    src_ref,
    sig_ref,
    te,
    to,
    xe,
    xo,
    got_ref,
    gust,
    plane,
    cos_ref,
    sin_ref,
    wave_ref,
    pick_ref,
    out_ref,
):
    place = where()
    step(1.0, place, stagger, a_theta, a_axial, a_radial, u_ref, base_ref, src_ref, sig_ref, te, to, xe, xo, out_ref)
    nhp, nvar, rows, nr = out_ref.shape
    nharm, nmode = plane.shape
    scale = 1.0 / math.sqrt(8 * tdevices * nr)
    last = (place[1] == xdevices - 1).astype(jnp.int32)
    holds = jnp.logical_or(place[1] == 0, place[1] == xdevices - 1)

    @pl.when(holds)
    def _():
        amp = jnp.sum(got_ref[...], axis=0)
        for h in range(nharm):
            cos, sin = cos_ref[h, 0:8], sin_ref[h, 0:8]
            mine = plane[h : h + 1, :] == last
            miss_re = jnp.where(mine, amp[2 * h : 2 * h + 1] - gust[h, 0:1, :], 0.0)
            miss_im = jnp.where(mine, amp[2 * h + 1 : 2 * h + 2] - gust[h, 1:2, :], 0.0)
            coef = jnp.concatenate([miss_re * cos - miss_im * sin, miss_re * sin + miss_im * cos], axis=0)
            nt = (((1,), (1,)), ((), ()))
            grouped = lax.dot_general(coef, pick_ref[h], nt, precision=highest, preferred_element_type=jnp.float32)
            q = scale * jnp.dot(grouped, wave_ref[...], precision=highest, preferred_element_type=jnp.float32)
            for p in range(2):
                for v in range(nvar):
                    at = pl.ds(last * 7, 8, stride=8)
                    out_ref[2 * h + p, v, at, :] = (
                        out_ref[2 * h + p, v, at, :] - r_cols[last, v] * q[p * 8 : (p + 1) * 8]
                    )


def call(kernel, name, scalars, arrays, outs, unread=0):
    single = not isinstance(outs, (list, tuple))
    out = pl.pallas_call(
        kernel,
        in_specs=[spec(SM)] * len(scalars)
        + [spec(VM)] * (len(arrays) - unread)
        + [spec(pl.ANY)] * unread,
        out_specs=spec(VM) if single else [spec(VM)] * len(outs),
        out_shape=outs,
        compiler_params=params(name),
        name=name,
    )(*scalars, *arrays)
    return out


def local(
    state, source, sigma, stagger, a_theta, a_axial, a_radial, mode_order, mode_radial, mode_plane, gust, l_rows, r_cols
):
    nharm, two, nvar, ctheta, caxial, nradial = state.shape
    nhp, nmode = nharm * two, mode_order.shape[1]
    tdev, xdev = lax.axis_size("theta"), lax.axis_size("xr")
    nrad = 8
    block = (nhp, nvar, ctheta * caxial, nradial)
    u = state.reshape(block)
    src = source.reshape(block)
    sig = sigma.reshape(ctheta * caxial, nradial)

    def array(*shape):
        return jax.ShapeDtypeStruct(shape, jnp.float32)

    face = array(nhp, nvar, 8, nradial)
    packed = array(nhp + 1, nvar, 8, nradial)
    whole = array(*block)

    even_t = [(i, i ^ 1) for i in range(tdev)]
    odd_t = [(i, (i + 1) % tdev if i % 2 else (i - 1) % tdev) for i in range(tdev)]
    even_x = [(i, i ^ 1) for i in range(xdev)]
    odd_x = [(i, i + 1 if i % 2 else i - 1) for i in range(1, xdev - 1)]

    def swap(te, to, xe, xo):
        return (
            lax.ppermute(te, "theta", even_t),
            lax.ppermute(to, "theta", odd_t),
            lax.ppermute(xe, "xr", even_x),
            lax.ppermute(xo, "xr", odd_x),
        )

    coefs = (stagger, a_theta, a_axial, a_radial)
    faces = call(pack_kernel, "pack_faces", (stagger,), (u, sig), [packed] * 2 + [face] * 2)
    faces = swap(*faces)
    *tabs, near = call(
        functools.partial(table_kernel, tdev, xdev),
        "mode_tables",
        (),
        (mode_order, mode_radial, u, src),
        [array(nharm, 16, nmode)] * 2
        + [array(nrad, nradial), array(nharm, nrad, nmode), array(5, nhp, nvar, 8, nradial)],
    )

    def planes(after):
        return call(
            functools.partial(plane_kernel, tdev, xdev),
            "plane_part",
            (*coefs, l_rows),
            (near, sig, faces[0], faces[1], mode_plane, *tabs, after, faces[2], faces[3]),
            array(tdev, 8, nmode),
            3,
        )

    def first_step(after):
        return call(first_kernel, "first_step", coefs, (u, src, sig, *faces, after), [whole] + [face] * 4, 1)

    if planes_first:
        part = planes(sigma)
        first, *faces2 = first_step(part)
    else:
        first, *faces2 = first_step(sigma)
        part = planes(first)
    got = lax.all_to_all(part, "theta", 0, 0, tiled=True)
    faces2 = swap(*faces2)
    amp = call(functools.partial(share_kernel, xdev), "share_amplitudes", (), (got,), array(xdev, 8, nmode))
    amp = lax.all_to_all(amp, "xr", 0, 0, tiled=True)
    fields = call(
        functools.partial(second_kernel, tdev, xdev),
        "second_step",
        (*coefs, r_cols),
        (first, u, src, sig, *faces2, got, gust, mode_plane, *tabs),
        whole,
    )
    amplitudes = call(finish_kernel, "finish_amplitudes", (), (amp, mode_plane), array(nharm, 2, two, nmode))
    return fields.reshape(state.shape), amplitudes


def solution(mesh):
    placed = (
        P(None, None, None, "theta", "xr", None),
        P(None, None, None, "theta", "xr", None),
        P("theta", "xr", None),
        P("theta"),
        P(),
        P(),
        P(),
        P(),
        P(),
        P(),
        P(),
        P(),
        P(),
    )
    return jax.shard_map(
        local,
        mesh=mesh,
        in_specs=placed,
        out_specs=(P(None, None, None, "theta", "xr", None), P()),
        check_vma=False,
    )
```

```python
import functools
import math

import jax
import jax.numpy as jnp
from jax import lax
from jax.experimental import pallas as pl
from jax.experimental.pallas import tpu as pltpu
from jax.sharding import PartitionSpec as P

courant = 0.5
viscosity = 0.1
base_frequency = 0.5
highest = lax.Precision.HIGHEST
VM = pltpu.VMEM
SM = pltpu.SMEM
planes_first = True
wide = ("pack_faces", "plane_part", "mode_tables", "first_step", "second_step")


def where():
    return lax.axis_index("theta"), lax.axis_index("xr")


def spec(space):
    return pl.BlockSpec(memory_space=space)


def params(name):
    size = 60 if name in wide else 16
    return pltpu.CompilerParams(vmem_limit_bytes=size * 1024 * 1024)


def write_faces(place, u_ref, te_ref, to_ref, xe_ref, xo_ref):
    nhp, nvar = u_ref.shape[0], u_ref.shape[1]
    todd = lax.rem(place[0], 2)
    xodd = lax.rem(place[1], 2)
    for out_ref, layer in ((te_ref, 1 - todd), (to_ref, todd)):
        start = pl.multiple_of(layer * 56, 8)
        out_ref[0:nhp] = u_ref[:, :, pl.ds(start, 8), :]
    for out_ref, row in ((xe_ref, 1 - xodd), (xo_ref, xodd)):
        for i in range(nhp):
            for v in range(nvar):
                out_ref[i, v] = u_ref[i, v, pl.ds(row * 7, 8, stride=8), :]


def pack_kernel(stagger, u_ref, sig_ref, te_ref, to_ref, xe_ref, xo_ref):
    place = where()
    write_faces(place, u_ref, te_ref, to_ref, xe_ref, xo_ref)
    nhp = u_ref.shape[0]
    nr = u_ref.shape[3]
    npass = stagger.shape[0]
    todd = lax.rem(place[0], 2)
    for out_ref, layer in ((te_ref, 1 - todd), (to_ref, todd)):
        start = pl.multiple_of(layer * 48, 8)
        out_ref[nhp, 0] = sig_ref[pl.ds(start, 8), :]
        out_ref[nhp, 1] = sig_ref[pl.ds(start + 8, 8), :]
        setting = stagger[layer * (npass - 1)].astype(jnp.float32)
        for i in range(2, out_ref.shape[1]):
            out_ref[nhp, i] = jnp.full((8, nr), setting, jnp.float32)


def step(factor, place, stagger, a_theta, a_axial, a_radial, u_ref, base_ref, src_ref, sig_ref, te, to, xe, xo, out_ref):
    nhp, nvar, rows, nr = u_ref.shape
    tcells = rows // 8
    cpp = tcells // stagger.shape[0]
    todd = lax.rem(place[0], 2) == 1
    xodd = lax.rem(place[1], 2) == 1
    shape = (nhp, 8, nr)
    row = lax.broadcasted_iota(jnp.int32, shape, 1)
    lane = lax.broadcasted_iota(jnp.int32, shape, 2)
    axial = [[0.5 * a_axial[v, w] for w in range(nvar)] for v in range(nvar)]
    radial = [[0.5 * a_radial[v, w] for w in range(nvar)] for v in range(nvar)]
    for t in range(tcells):
        setting = stagger[t // cpp]
        tile = slice(8 * t, 8 * t + 8)
        sig = sig_ref[tile, :][None]
        own = sig + 6.0 * viscosity
        scaled = (factor * courant) / (1.0 + sig)
        acc = [None] * nvar
        for w in range(nvar):
            u = u_ref[:, w, tile, :]
            if t == 0:
                tm = jnp.where(todd, te[0:nhp, w], to[0:nhp, w])
            else:
                tm = u_ref[:, w, 8 * t - 8 : 8 * t, :]
            if t == tcells - 1:
                tp = jnp.where(todd, to[0:nhp, w], te[0:nhp, w])
            else:
                tp = u_ref[:, w, 8 * t + 8 : 8 * t + 16, :]
            e = xe[:, w, t : t + 1, :]
            o = xo[:, w, t : t + 1, :]
            xlo = jnp.where(xodd, e, o)
            xhi = jnp.where(xodd, o, e)
            xm = jnp.where(row == 0, jnp.broadcast_to(xlo, shape), pltpu.roll(u, 1, 1))
            xp = jnp.where(row == 7, jnp.broadcast_to(xhi, shape), pltpu.roll(u, 7, 1))
            rm = jnp.where(lane == 0, 0.0, pltpu.roll(u, 1, 2))
            rp = jnp.where(lane == nr - 1, 0.0, pltpu.roll(u, nr - 1, 2))
            dt_, dx_, dr_ = tp - tm, xp - xm, rp - rm
            near = ((tp + tm) + (xp + xm)) + (rp + rm)
            turned = []
            for h in range(nhp // 2):
                freq = base_frequency * (1.0 + h)
                turned.append(-freq * u[2 * h + 1 : 2 * h + 2])
                turned.append(freq * u[2 * h : 2 * h + 1])
            local_part = (own * u - viscosity * near) + (jnp.concatenate(turned, axis=0) - src_ref[:, w, tile, :])
            for v in range(nvar):
                flux = (0.5 * a_theta[setting, v, w]) * dt_ + axial[v][w] * dx_ + radial[v][w] * dr_
                if v == w:
                    flux = flux + local_part
                acc[v] = flux if acc[v] is None else acc[v] + flux
        for v in range(nvar):
            out_ref[:, v, tile, :] = base_ref[:, v, tile, :] - scaled * acc[v]


def first_kernel(stagger, a_theta, a_axial, a_radial, u_ref, src_ref, sig_ref, te, to, xe, xo, after, out_ref, te2, to2, xe2, xo2
):
    place = where()
    step(0.5, place, stagger, a_theta, a_axial, a_radial, u_ref, u_ref, src_ref, sig_ref, te, to, xe, xo, out_ref)
    write_faces(place, out_ref, te2, to2, xe2, xo2)


def table_kernel(
    tdevices, xdevices, order, radial, u_ref, src_ref, cos_ref, sin_ref, wave_ref, pick_ref, rows_ref
):
    place = where()
    last = (place[1] == xdevices - 1).astype(jnp.int32)
    for ref, first_slot, count in ((u_ref, 0, 3), (src_ref, 3, 2)):
        for j in range(count):
            at = pl.ds(last * 7 + j * (1 - 2 * last), 8, stride=8)
            for i in range(u_ref.shape[0]):
                for v in range(u_ref.shape[1]):
                    rows_ref[first_slot + j, i, v] = ref[i, v, at, :]
    nharm, nmode = order.shape
    tcells = 8
    total = tcells * tdevices
    row = lax.broadcasted_iota(jnp.int32, (2 * tcells, nmode), 0)
    cell = place[0] * tcells + jnp.where(row < 12, row, row - 16)
    nrad, nr = wave_ref.shape
    wave_ref[...] = radial_table(nrad, nr)
    for h in range(nharm):
        turns = lax.rem(order[h : h + 1, :] * cell + 64 * total, total)
        angle = 2.0 * math.pi * turns.astype(jnp.float32) / total
        cos_ref[h] = jnp.cos(angle)
        sin_ref[h] = jnp.sin(angle)
        n = lax.broadcasted_iota(jnp.int32, (nrad, nmode), 0)
        pick_ref[h] = (n == radial[h : h + 1, :]).astype(jnp.float32)


def radial_table(nrad, nr):
    n = lax.broadcasted_iota(jnp.int32, (nrad, nr), 0)
    pos = lax.broadcasted_iota(jnp.int32, (nrad, nr), 1).astype(jnp.float32) + 0.5
    wave = math.sqrt(2.0) * jnp.cos(math.pi * n.astype(jnp.float32) * pos / nr)
    return jnp.where(n == 0, 1.0, wave)


def turn(u):
    out = []
    for h in range(u.shape[0] // 2):
        freq = base_frequency * (1.0 + h)
        out.append(-freq * u[2 * h + 1 : 2 * h + 2])
        out.append(freq * u[2 * h : 2 * h + 1])
    return jnp.concatenate(out, axis=0)


def plane_part(last, tdevices, stagger, a_theta, a_axial, a_radial, l_rows, rows_ref, sig_ref, lo, hi, refs):
    plane, cos_ref, sin_ref, wave_ref, pick_ref, part_ref = refs
    _, nhp, nvar, _, nr = rows_ref.shape
    nharm, nmode = plane.shape
    nset = a_theta.shape[0]
    scale = 1.0 / math.sqrt(8 * tdevices * nr)
    shape = (nhp, 8, nr)
    row = lax.broadcasted_iota(jnp.int32, shape, 1)
    lane = lax.broadcasted_iota(jnp.int32, shape, 2)
    row1, row2 = row[0], lax.broadcasted_iota(jnp.int32, (8, nr), 0)
    side = (1 - 2 * last).astype(jnp.float32)
    at = [last * 7 + j * (1 - 2 * last) for j in range(3)]

    def shift_r(u):
        return (
            jnp.where(lane == 0, 0.0, pltpu.roll(u, 1, 2)),
            jnp.where(lane == nr - 1, 0.0, pltpu.roll(u, nr - 1, 2)),
        )

    def row_of(face, i, j):
        return jnp.broadcast_to(face(i, pl.ds(at[j], 1)), (8, nr))

    settings = jnp.where(row2 < 4, hi(2, slice(0, 8)), lo(2, slice(0, 8)))
    table = [[None] * nvar for _ in range(nvar)]
    outer = [[None] * nvar for _ in range(nvar)]
    for v in range(nvar):
        for w in range(nvar):
            table[v][w] = jnp.where(row2 < 4, 0.5 * a_theta[stagger[0], v, w], 0.5 * a_theta[stagger[1], v, w])[None]
            value = jnp.full((8, nr), 0.5 * a_theta[nset - 1, v, w], jnp.float32)
            for s in range(nset - 1):
                value = jnp.where(settings == float(s), 0.5 * a_theta[s, v, w], value)
            outer[v][w] = value[None]
    axial = [[0.5 * side * a_axial[v, w] for w in range(nvar)] for v in range(nvar)]
    radial = [[0.5 * a_radial[v, w] for w in range(nvar)] for v in range(nvar)]
    weight = [l_rows[last, v] for v in range(nvar)]

    sig, sig_out, step_in, step_out = [], [], [], []
    for j in range(2):
        sig.append(sig_ref[pl.ds(at[j], 8, stride=8), :][None])
        edge = jnp.where(row2 == 0, row_of(hi, 0, j), row_of(hi, 1, j))
        edge = jnp.where(row2 == 6, row_of(lo, 0, j), edge)
        edge = jnp.where(row2 == 7, row_of(lo, 1, j), edge)
        sig_out.append(edge[None])
        step_in.append(courant / (1.0 + sig[j]))
        step_out.append(courant / (1.0 + sig_out[j]))

    state = [[rows_ref[j, :, v] for v in range(nvar)] for j in range(3)]
    source = [[rows_ref[3 + j, :, v] for v in range(nvar)] for j in range(2)]
    first, first_out = [], []
    for j in range(2):
        acc, acc_out = [None] * nvar, [None] * nvar
        for w in range(nvar):
            u = state[j][w]
            up, down = pltpu.roll(u, 7, 1), pltpu.roll(u, 1, 1)
            tp, tm = jnp.where(row == 7, 0.0, up), jnp.where(row == 0, 0.0, down)
            tp_out, tm_out = jnp.where(row == 7, up, 0.0), jnp.where(row == 0, down, 0.0)
            rm, rp = shift_r(u)
            inner = state[j + 1][w]
            if j == 0:
                dx_, nx = inner, inner
            else:
                dx_, nx = inner - state[0][w], inner + state[0][w]
            dt_, dr_ = tp - tm, rp - rm
            dt_out = tp_out - tm_out
            near = (tp + tm) + nx + (rp + rm)
            part = ((sig[j] + 6.0 * viscosity) * u - viscosity * near) + (turn(u) - source[j][w])
            for v in range(nvar):
                flux = table[v][w] * dt_ + axial[v][w] * dx_ + radial[v][w] * dr_
                flux_out = outer[v][w] * dt_out
                if v == w:
                    flux = flux + part
                    flux_out = flux_out - viscosity * (tp_out + tm_out)
                acc[v] = flux if acc[v] is None else acc[v] + flux
                acc_out[v] = flux_out if acc_out[v] is None else acc_out[v] + flux_out
        first.append([state[j][v] - (0.5 * step_in[j]) * acc[v] for v in range(nvar)])
        first_out.append([-(0.5 * step_out[j]) * acc_out[v] for v in range(nvar)])

    zero = jnp.zeros(shape, jnp.float32)
    base, total, total_out, mean, mean_out = zero, zero, zero, zero, zero
    for w in range(nvar):
        f, g = first[0][w], first_out[0][w]
        fd, fu, gd, gu = pltpu.roll(f, 1, 1), pltpu.roll(f, 7, 1), pltpu.roll(g, 1, 1), pltpu.roll(g, 7, 1)
        lt = sum(weight[v] * table[v][w] for v in range(nvar))
        lt_out = sum(weight[v] * outer[v][w] for v in range(nvar))
        lx = sum(weight[v] * axial[v][w] for v in range(nvar))
        lr = sum(weight[v] * radial[v][w] for v in range(nvar))
        for inside in (True, False):
            here, beside = (f, first[1][w]) if inside else (g, first_out[1][w])
            if inside:
                tm, tp = jnp.where(row == 0, gd, fd), jnp.where(row == 7, gu, fu)
            else:
                tm, tp = jnp.where(row == 0, fd, gd), jnp.where(row == 7, fu, gu)
            rm, rp = shift_r(here)
            near = (tp + tm) + beside + (rp + rm)
            term = (lt if inside else lt_out) * (tp - tm) + lx * beside + lr * (rp - rm)
            s = (sig if inside else sig_out)[0] + 6.0 * viscosity
            if inside:
                total = total + term + weight[w] * ((s * here - viscosity * near) - source[0][w])
                mean = mean + weight[w] * here
                base = base + weight[w] * state[0][w]
            else:
                total_out = total_out + term + weight[w] * (s * here - viscosity * near)
                mean_out = mean_out + weight[w] * here
    values = base - step_in[0] * (total + turn(mean))
    values_out = -step_out[0] * (total_out + turn(mean_out))
    values = jnp.stack([values, values_out], axis=1).reshape(nhp * 16, nr)
    nt = (((1,), (1,)), ((), ()))
    grouped = lax.dot_general(values, wave_ref[...], nt, precision=highest, preferred_element_type=jnp.float32)
    for h in range(nharm):
        mine = plane[h : h + 1, :] == last
        both = jnp.dot(
            grouped[32 * h : 32 * h + 32], pick_ref[h], precision=highest, preferred_element_type=jnp.float32
        )
        re, im = both[:16], both[16:]
        cos, sin = cos_ref[h], sin_ref[h]
        part_re = scale * jnp.sum(re * cos + im * sin, axis=0, keepdims=True)
        part_im = scale * jnp.sum(im * cos - re * sin, axis=0, keepdims=True)
        part_re, part_im = jnp.where(mine, part_re, 0.0), jnp.where(mine, part_im, 0.0)
        part_ref[:, 2 * h] = jnp.broadcast_to(part_re, (tdevices, nmode))
        part_ref[:, 2 * h + 1] = jnp.broadcast_to(part_im, (tdevices, nmode))
    part_ref[:, nhp:] = jnp.zeros((tdevices, 8 - nhp, nmode), jnp.float32)


def plane_kernel(
    tdevices,
    xdevices,
    stagger,
    a_theta,
    a_axial,
    a_radial,
    l_rows,
    rows_ref,
    sig_ref,
    te,
    to,
    plane,
    cos_ref,
    sin_ref,
    wave_ref,
    pick_ref,
    after,
    after2,
    after3,
    part_ref,
):
    place = where()
    nhp = rows_ref.shape[1]
    last = (place[1] == xdevices - 1).astype(jnp.int32)
    holds = jnp.logical_or(place[1] == 0, place[1] == xdevices - 1)
    todd = lax.rem(place[0], 2) == 1

    def lo(i, rows):
        return jnp.where(todd, te[nhp, i, rows, :], to[nhp, i, rows, :])

    def hi(i, rows):
        return jnp.where(todd, to[nhp, i, rows, :], te[nhp, i, rows, :])

    @pl.when(holds)
    def _():
        refs = (plane, cos_ref, sin_ref, wave_ref, pick_ref, part_ref)
        plane_part(
            last, tdevices, stagger, a_theta, a_axial, a_radial, l_rows, rows_ref, sig_ref, lo, hi, refs
        )

    @pl.when(jnp.logical_not(holds))
    def _():
        part_ref[...] = jnp.zeros(part_ref.shape, jnp.float32)


def share_kernel(xdevices, got_ref, amp_ref):
    amp = jnp.sum(got_ref[...], axis=0)
    for d in range(xdevices):
        amp_ref[d] = amp


def finish_kernel(got_ref, plane, out_ref):
    amp = jnp.sum(got_ref[...], axis=0)
    for h in range(plane.shape[0]):
        for b in range(2):
            out_ref[h, b] = jnp.where(plane[h : h + 1, :] == b, amp[2 * h : 2 * h + 2], 0.0)


def second_kernel(
    tdevices,
    xdevices,
    stagger,
    a_theta,
    a_axial,
    a_radial,
    r_cols,
    u_ref,
    base_ref,
    src_ref,
    sig_ref,
    te,
    to,
    xe,
    xo,
    got_ref,
    gust,
    plane,
    cos_ref,
    sin_ref,
    wave_ref,
    pick_ref,
    out_ref,
):
    place = where()
    step(1.0, place, stagger, a_theta, a_axial, a_radial, u_ref, base_ref, src_ref, sig_ref, te, to, xe, xo, out_ref)
    nhp, nvar, rows, nr = out_ref.shape
    nharm, nmode = plane.shape
    scale = 1.0 / math.sqrt(8 * tdevices * nr)
    last = (place[1] == xdevices - 1).astype(jnp.int32)
    holds = jnp.logical_or(place[1] == 0, place[1] == xdevices - 1)

    @pl.when(holds)
    def _():
        amp = got_ref[0]
        for h in range(nharm):
            cos, sin = cos_ref[h, 0:8], sin_ref[h, 0:8]
            mine = plane[h : h + 1, :] == last
            miss_re = jnp.where(mine, amp[2 * h : 2 * h + 1] - gust[h, 0:1, :], 0.0)
            miss_im = jnp.where(mine, amp[2 * h + 1 : 2 * h + 2] - gust[h, 1:2, :], 0.0)
            coef = jnp.concatenate([miss_re * cos - miss_im * sin, miss_re * sin + miss_im * cos], axis=0)
            nt = (((1,), (1,)), ((), ()))
            grouped = lax.dot_general(coef, pick_ref[h], nt, precision=highest, preferred_element_type=jnp.float32)
            q = scale * jnp.dot(grouped, wave_ref[...], precision=highest, preferred_element_type=jnp.float32)
            for p in range(2):
                for v in range(nvar):
                    at = pl.ds(last * 7, 8, stride=8)
                    out_ref[2 * h + p, v, at, :] = (
                        out_ref[2 * h + p, v, at, :] - r_cols[last, v] * q[p * 8 : (p + 1) * 8]
                    )


def call(kernel, name, scalars, arrays, outs, unread=0):
    single = not isinstance(outs, (list, tuple))
    out = pl.pallas_call(
        kernel,
        in_specs=[spec(SM)] * len(scalars)
        + [spec(VM)] * (len(arrays) - unread)
        + [spec(pl.ANY)] * unread,
        out_specs=spec(VM) if single else [spec(VM)] * len(outs),
        out_shape=outs,
        compiler_params=params(name),
        name=name,
    )(*scalars, *arrays)
    return out


def local(
    state, source, sigma, stagger, a_theta, a_axial, a_radial, mode_order, mode_radial, mode_plane, gust, l_rows, r_cols
):
    nharm, two, nvar, ctheta, caxial, nradial = state.shape
    nhp, nmode = nharm * two, mode_order.shape[1]
    tdev, xdev = lax.axis_size("theta"), lax.axis_size("xr")
    nrad = 8
    block = (nhp, nvar, ctheta * caxial, nradial)
    u = state.reshape(block)
    src = source.reshape(block)
    sig = sigma.reshape(ctheta * caxial, nradial)

    def array(*shape):
        return jax.ShapeDtypeStruct(shape, jnp.float32)

    face = array(nhp, nvar, 8, nradial)
    packed = array(nhp + 1, nvar, 8, nradial)
    whole = array(*block)

    even_t = [(i, i ^ 1) for i in range(tdev)]
    odd_t = [(i, (i + 1) % tdev if i % 2 else (i - 1) % tdev) for i in range(tdev)]
    even_x = [(i, i ^ 1) for i in range(xdev)]
    odd_x = [(i, i + 1 if i % 2 else i - 1) for i in range(1, xdev - 1)]

    def swap(te, to, xe, xo):
        return (
            lax.ppermute(te, "theta", even_t),
            lax.ppermute(to, "theta", odd_t),
            lax.ppermute(xe, "xr", even_x),
            lax.ppermute(xo, "xr", odd_x),
        )

    coefs = (stagger, a_theta, a_axial, a_radial)
    faces = call(pack_kernel, "pack_faces", (stagger,), (u, sig), [packed] * 2 + [face] * 2)
    faces = swap(*faces)
    *tabs, near = call(
        functools.partial(table_kernel, tdev, xdev),
        "mode_tables",
        (),
        (mode_order, mode_radial, u, src),
        [array(nharm, 16, nmode)] * 2
        + [array(nrad, nradial), array(nharm, nrad, nmode), array(5, nhp, nvar, 8, nradial)],
    )

    def planes(after):
        return call(
            functools.partial(plane_kernel, tdev, xdev),
            "plane_part",
            (*coefs, l_rows),
            (near, sig, faces[0], faces[1], mode_plane, *tabs, after, faces[2], faces[3]),
            array(tdev, 8, nmode),
            3,
        )

    def first_step(after):
        return call(first_kernel, "first_step", coefs, (u, src, sig, *faces, after), [whole] + [face] * 4, 1)

    if planes_first:
        part = planes(sigma)
        first, *faces2 = first_step(part)
    else:
        first, *faces2 = first_step(sigma)
        part = planes(first)
    got = lax.all_to_all(part, "theta", 0, 0, tiled=True)
    faces2 = swap(*faces2)
    amp = call(functools.partial(share_kernel, xdev), "share_amplitudes", (), (got,), array(xdev, 8, nmode))
    mine = amp
    amp = lax.all_to_all(amp, "xr", 0, 0, tiled=True)
    fields = call(
        functools.partial(second_kernel, tdev, xdev),
        "second_step",
        (*coefs, r_cols),
        (first, u, src, sig, *faces2, mine, gust, mode_plane, *tabs),
        whole,
    )
    amplitudes = call(finish_kernel, "finish_amplitudes", (), (amp, mode_plane), array(nharm, 2, two, nmode))
    return fields.reshape(state.shape), amplitudes


def solution(mesh):
    placed = (
        P(None, None, None, "theta", "xr", None),
        P(None, None, None, "theta", "xr", None),
        P("theta", "xr", None),
        P("theta"),
        P(),
        P(),
        P(),
        P(),
        P(),
        P(),
        P(),
        P(),
        P(),
    )
    return jax.shard_map(
        local,
        mesh=mesh,
        in_specs=placed,
        out_specs=(P(None, None, None, "theta", "xr", None), P()),
        check_vma=False,
    )
```
